128 devices in a mesh: pair: 32 (over z_lo, x, y), row: 4 (over z_hi, core).
Axes of the slice: x: 4, y: 4, z: 4 (z_hi: 2, z_lo: 2; z = z_hi * 2 + z_lo), core: 2. Of those that a mesh axis runs over, the one named last changes fastest.
Arguments:
- factor: float32 [16384, 16384], P('row', 'pair'), may hold values from -90 to 90
Outputs:
- rotated: float32 [16384, 16384], P('row', 'pair')
The draws below stay inside these ranges and needn't reach their ends.
All inputs are finite; a program needn't handle non-finite values.
Results may differ from the reference program's by a relative error of at most 0.0003.
Values sent between devices are 32-bit elements; how exact they have to be, the bound alone decides.
No kernel may reach another device: no remote copies, remote signals or barrier semaphores. Data moves between devices by JAX's collectives and lax.ppermute only.
A program may use at most 128 MiB of HBM per device.

```python
import math
import jax
import jax.numpy as jnp
from jax import lax

N = 16384
B = 128
STEPS = 4
ITERS = 12
PAIRS = 64


def draw_factor(key, part):
    key = jax.random.fold_in(key, 11)
    keys = jax.random.split(key, 4)
    noise = jnp.clip(jax.random.normal(keys[0], (N, N), jnp.float32), -6.0, 6.0)
    row_scale = jnp.ones((N, 1), jnp.float32)
    common = jnp.clip(jax.random.normal(keys[1], (N, 1), jnp.float32), -6.0, 6.0)
    loads = jax.random.uniform(keys[2], (1, N), jnp.float32, 0.5, 1.5)
    column_scale = jnp.exp(jax.random.uniform(keys[3], (1, N), jnp.float32, math.log(0.3), math.log(3.0)))
    return (row_scale * column_scale * (noise + 0.6 * common * loads)).astype(jnp.float32)


def setup_inputs(seed: int = 0) -> dict:
    seeds = jax.random.split(jax.random.key(seed), 2)
    return {
        "factor": draw_factor(jax.random.fold_in(seeds[1], 71), 0),
    }


EPS = 1e-06
DAMPING = 0.04
HIGH = lax.Precision.HIGHEST

def coupling_from(gram, norm_top, norm_bottom):
    differ = norm_top[:, :, None] - norm_bottom[:, None, :]
    total = norm_top[:, :, None] + norm_bottom[:, None, :] + EPS
    radius = jnp.sqrt(differ * differ + 4.0 * gram * gram)
    denominator = differ * differ + jnp.abs(differ) * radius + DAMPING * total * total
    return -2.0 * gram * differ / denominator

def polar_from(coupling):
    eye = jnp.eye(coupling.shape[0], dtype=jnp.float32)
    upper = jnp.concatenate([eye, coupling], axis=1)
    lower = jnp.concatenate([-coupling.T, eye], axis=1)
    scale = lax.rsqrt(1.0 + jnp.sum(coupling * coupling))
    matrix = jnp.concatenate([upper, lower], axis=0) * scale
    for index in range(ITERS):
        inner = jnp.dot(matrix.T, matrix, precision=HIGH)
        matrix = 1.5 * matrix - 0.5 * jnp.dot(matrix, inner, precision=HIGH)
    return matrix

def reference(factor):
    joined = factor.reshape(N, PAIRS, 2 * B)
    for step in range(STEPS):
        top = joined[:, :, :B]
        bottom = joined[:, :, B:]
        gram = jnp.einsum('mpi,mpj->pij', top, bottom, precision=HIGH)
        norm_top = lax.optimization_barrier(jnp.sum(top * top, axis=0))
        norm_bottom = lax.optimization_barrier(jnp.sum(bottom * bottom, axis=0))
        coupling = coupling_from(gram, norm_top, norm_bottom)
        polar = jax.vmap(polar_from)(coupling)
        joined = jnp.einsum('mpa,pab->mpb', joined, polar, precision=HIGH)
        if step < STEPS - 1:
            top = joined[:, :, :B]
            bottom = joined[:, :, B:]
            new_top = jnp.concatenate([top[:, :1], bottom[:, :1], top[:, 1:-1]], axis=1)
            new_bottom = jnp.concatenate([bottom[:, 1:], top[:, -1:]], axis=1)
            joined = jnp.concatenate([new_top, new_bottom], axis=2)
    return joined.reshape(N, N)
```

```python
import functools
import jax
import jax.numpy as jnp
from jax import lax
from jax.experimental import pallas as pl
from jax.experimental.pallas import tpu as pltpu
from jax.sharding import PartitionSpec as P

B = 128
STEPS = 4
ITERS = 12
EPS = 1e-06
DAMPING = 0.04
CHUNKS = 1
TILE = 512
GROWS = 136
F32 = jnp.float32
BF16 = jnp.bfloat16
PARAMS = pltpu.CompilerParams(vmem_limit_bytes=40 * 1024 * 1024)
NN = (((1,), (0,)), ((), ()))
NT = (((1,), (1,)), ((), ()))
TN = (((0,), (0,)), ((), ()))


def halves(value):
    high = value.astype(BF16)
    return high, (value - high.astype(F32)).astype(BF16)


def dot(a, b, dims=NN):
    return lax.dot_general(a, b, dims, preferred_element_type=F32)


def dot3(a, b, dims=NN):
    return dot(a[0], b[0], dims) + (dot(a[0], b[1], dims) + dot(a[1], b[0], dims))


def beside(a, b):
    return jnp.concatenate([a, b], axis=1)


def add_gram(g_ref, pair, top, bottom):
    product = dot(beside(*halves(top)), beside(*halves(bottom)), TN)
    g_ref[pair, :B, :] += (product[:B, :B] + product[B:, B:]) + (product[:B, B:] + product[B:, :B])
    g_ref[pair, B : B + 1, :] += jnp.sum(top * top, axis=0, keepdims=True)
    g_ref[pair, B + 1 : B + 2, :] += jnp.sum(bottom * bottom, axis=0, keepdims=True)


def gram_first_kernel(x_ref, g_ref):
    @pl.when(pl.program_id(0) == 0)
    def _():
        g_ref[...] = jnp.zeros_like(g_ref)

    for pair in range(2):
        base = 2 * B * pair
        add_gram(g_ref, pair, x_ref[:, base : base + B], x_ref[:, base + B : base + 2 * B])


def gram_first(x):
    rows = x.shape[0]
    tile = min(TILE, rows)
    return pl.pallas_call(
        gram_first_kernel,
        grid=(rows // tile,),
        in_specs=[pl.BlockSpec((tile, 4 * B), lambda i: (i, 0))],
        out_specs=pl.BlockSpec((2, GROWS, B), lambda i: (0, 0, 0)),
        out_shape=jax.ShapeDtypeStruct((2, GROWS, B), F32),
        compiler_params=PARAMS,
        name="gram_first",
    )(x)


def gram_next_kernel(rebuild, flag_ref, first_ref, last_ref, b0_ref, t1_ref, in_top_ref, in_bottom_ref, *rest):
    if rebuild:
        prev_left_ref, prev_right_ref, q_top_ref, q_bottom_ref, g_in_ref, g_ref, t0_ref, b1_ref = rest
    else:
        g_in_ref, g_ref, t0_ref, b1_ref = rest

    @pl.when(pl.program_id(0) == 0)
    def _():
        g_ref[...] = g_in_ref[...]

    in_top, in_bottom = in_top_ref[...], in_bottom_ref[...]
    if rebuild:
        in_top = dot3(halves(beside(in_top, prev_left_ref[...])), halves(q_top_ref[...]))
        in_bottom = dot3(halves(beside(prev_right_ref[...], in_bottom)), halves(q_bottom_ref[...]))
    t0 = jnp.where(flag_ref[0] == 1, first_ref[...], in_top)
    b1 = jnp.where(flag_ref[1] == 1, last_ref[...], in_bottom)
    t0_ref[...] = t0
    b1_ref[...] = b1
    add_gram(g_ref, 0, t0, b0_ref[...])
    add_gram(g_ref, 1, t1_ref[...], b1)


def gram_next(flags, blocks, rebuilt, g_in):
    rows = blocks[0].shape[0]
    tile = min(TILE, rows)
    block = pl.BlockSpec((tile, B), lambda i: (i, 0))
    half = pl.BlockSpec((2 * B, B), lambda i: (0, 0))
    gram = pl.BlockSpec((2, GROWS, B), lambda i: (0, 0, 0))
    extra = [block, block, half, half] if rebuilt else []
    return pl.pallas_call(
        functools.partial(gram_next_kernel, bool(rebuilt)),
        grid=(rows // tile,),
        in_specs=[pl.BlockSpec(memory_space=pltpu.SMEM)] + [block] * 6 + extra + [gram],
        out_specs=[gram, block, block],
        out_shape=[jax.ShapeDtypeStruct((2, GROWS, B), F32)] + [jax.ShapeDtypeStruct((rows, B), F32)] * 2,
        compiler_params=PARAMS,
        name="gram_next",
    )(flags, *blocks, *rebuilt, g_in)


def polar_kernel(g0_ref, g1_ref, g2_ref, g3_ref, q_ref, right_ref, left_ref):
    total = (g0_ref[...] + g1_ref[...]) + (g2_ref[...] + g3_ref[...])
    eye = (lax.broadcasted_iota(jnp.int32, (B, B), 0) == lax.broadcasted_iota(jnp.int32, (B, B), 1)).astype(F32)
    chains = []
    for pair in range(2):
        gram = total[pair, :B]
        norm_top = jnp.transpose(jnp.broadcast_to(total[pair, B : B + 1], (B, B)))
        norm_bottom = jnp.broadcast_to(total[pair, B + 1 : B + 2], (B, B))
        differ = norm_top - norm_bottom
        both = norm_top + norm_bottom + EPS
        radius = jnp.sqrt(differ * differ + 4.0 * gram * gram)
        denominator = differ * differ + jnp.abs(differ) * radius + DAMPING * both * both
        coupling = -2.0 * gram * differ / denominator
        scale = lax.rsqrt(1.0 + jnp.sum(coupling * coupling, keepdims=True))
        chains.append(beside(eye, coupling) * scale)
        chains.append(beside(-jnp.transpose(coupling), eye) * scale)

    def iterate(_, chains):
        parts = [halves(chain) for chain in chains]
        inner = [halves(dot3(part, part, NT)) for part in parts]
        return tuple(1.5 * chain - 0.5 * dot3(m, part) for chain, m, part in zip(chains, inner, parts))

    chains = lax.fori_loop(0, ITERS, iterate, tuple(chains))
    for pair in range(2):
        q_ref[pair, :B, :] = chains[2 * pair]
        q_ref[pair, B:, :] = chains[2 * pair + 1]
    right_ref[:B, :] = chains[2][:, :B]
    right_ref[B:, :] = chains[3][:, :B]
    left_ref[:B, :] = chains[0][:, B:]
    left_ref[B:, :] = chains[1][:, B:]


def polar(grams):
    return pl.pallas_call(
        polar_kernel,
        out_shape=[
            jax.ShapeDtypeStruct((2, 2 * B, 2 * B), F32),
            jax.ShapeDtypeStruct((2 * B, B), F32),
            jax.ShapeDtypeStruct((2 * B, B), F32),
        ],
        compiler_params=PARAMS,
        name="polar",
    )(*grams)


def rotate_kernel(whole, last, flag_ref, *refs):
    if whole:
        x_ref, q_ref, *outs = refs
        pairs = [x_ref[:, : 2 * B], x_ref[:, 2 * B :]]
    else:
        t0_ref, b0_ref, t1_ref, b1_ref, q_ref, *outs = refs
        pairs = [beside(t0_ref[...], b0_ref[...]), beside(t1_ref[...], b1_ref[...])]
    turned = [dot3(halves(pairs[k]), halves(q_ref[k])) for k in range(2)]
    if last:
        outs[0][:, : 2 * B] = turned[0]
        outs[0][:, 2 * B :] = turned[1]
        return
    right_ref, left_ref, t1n_ref, b0n_ref = outs
    first = flag_ref[0] == 1
    t0, b0 = turned[0][:, :B], turned[0][:, B:]
    right_ref[...] = turned[1][:, :B]
    left_ref[...] = jnp.where(first, t0, b0)
    t1n_ref[...] = jnp.where(first, b0, t0)
    b0n_ref[...] = turned[1][:, B:]


def rotate(flags, blocks, q, last=False, rows=None, start=0):
    whole = len(blocks) == 1
    rows = rows or blocks[0].shape[0]
    tile = min(TILE, rows)
    offset = start // tile
    block = pl.BlockSpec((tile, B), lambda i: (i, 0))
    wide = pl.BlockSpec((tile, 4 * B), lambda i: (i + offset, 0))
    full = pl.BlockSpec((2, 2 * B, 2 * B), lambda i: (0, 0, 0))
    if last:
        out_specs, out_shape = wide, jax.ShapeDtypeStruct((rows, 4 * B), F32)
    else:
        out_specs, out_shape = [block] * 4, [jax.ShapeDtypeStruct((rows, B), F32)] * 4
    return pl.pallas_call(
        functools.partial(rotate_kernel, whole, last),
        grid=(rows // tile,),
        in_specs=[pl.BlockSpec(memory_space=pltpu.SMEM)] + ([wide] if whole else [block] * 4) + [full],
        out_specs=out_specs,
        out_shape=out_shape,
        compiler_params=PARAMS,
        name="rotate",
    )(flags, *blocks, q)


def shifted(value, steps):
    count = lax.axis_size("pair")
    initial, last = (max(0, -steps), min(count, count - steps))
    return lax.ppermute(value, "pair", [(source, source + steps) for source in range(initial, last)])


def row_terms(value):
    count = lax.axis_size("row")
    return [value] + [lax.ppermute(value, "row", [(i, i ^ k) for i in range(count)]) for k in range(1, count)]


def after(values, done):
    return lax.optimization_barrier((values, done))


def per_device(factor):
    position = lax.axis_index("pair")
    flags = jnp.stack([position == 0, position == lax.axis_size("pair") - 1]).astype(jnp.int32)
    zero = jnp.zeros((2, GROWS, B), F32)

    q, _, _ = polar(row_terms(gram_first(factor)))
    right, left, t1, b0 = rotate(flags, [factor], q)
    arrived = (shifted(right, 1), shifted(left, -1))
    (t1, b0), arrived = after((t1, b0), arrived)
    ahead = (shifted(t1, 1), shifted(b0, -1))
    previous = (left, right)
    rebuilt = ()
    for step in range(1, STEPS):
        g, t0, b1 = gram_next(flags, (left, right, b0, t1, *arrived), rebuilt, zero)
        q, q_right, q_left = polar(row_terms(g))
        if step == STEPS - 1:
            return rotate(flags, [t0, b0, t1, b1], q, last=True)
        q_top, q_bottom = shifted(q_right, 1), shifted(q_left, -1)
        older = previous
        right, left, t1, b0 = rotate(flags, [t0, b0, t1, b1], q)
        previous = (left, right)
        rebuilt = (*older, q_top, q_bottom)
        arrived = ahead
        if step < STEPS - 2:
            (t1, b0), arrived = after((t1, b0), arrived)
            ahead = (shifted(t1, 1), shifted(b0, -1))


def solution(mesh):
    placed = (P("row", "pair"),)
    return jax.shard_map(
        per_device, mesh=mesh, in_specs=placed, out_specs=P("row", "pair"), check_vma=False
    )
```

```python
import functools
import jax
import jax.numpy as jnp
from jax import lax
from jax.experimental import pallas as pl
from jax.experimental.pallas import tpu as pltpu
from jax.sharding import PartitionSpec as P

B = 128
STEPS = 4
ITERS = 12
EPS = 1e-06
DAMPING = 0.04
TILE = 512
GROWS = 136
RELAY = 5
F32 = jnp.float32
BF16 = jnp.bfloat16
PARAMS = pltpu.CompilerParams(vmem_limit_bytes=40 * 1024 * 1024)
NN = (((1,), (0,)), ((), ()))
NT = (((1,), (1,)), ((), ()))
TN = (((0,), (0,)), ((), ()))


def halves(value):
    high = value.astype(BF16)
    return high, (value - high.astype(F32)).astype(BF16)


def dot(a, b, dims=NN):
    return lax.dot_general(a, b, dims, preferred_element_type=F32)


def dot3(a, b, dims=NN):
    return dot(a[0], b[0], dims) + (dot(a[0], b[1], dims) + dot(a[1], b[0], dims))


def beside(a, b):
    return jnp.concatenate([a, b], axis=1)


def add_gram(g_ref, pair, top, bottom):
    product = dot(beside(*halves(top)), beside(*halves(bottom)), TN)
    g_ref[pair, :B, :] += (product[:B, :B] + product[B:, B:]) + (product[:B, B:] + product[B:, :B])
    g_ref[pair, B : B + 1, :] += jnp.sum(top * top, axis=0, keepdims=True)
    g_ref[pair, B + 1 : B + 2, :] += jnp.sum(bottom * bottom, axis=0, keepdims=True)


def gram_first_kernel(x_ref, g_ref):
    @pl.when(pl.program_id(0) == 0)
    def _():
        g_ref[...] = jnp.zeros_like(g_ref)

    for pair in range(2):
        base = 2 * B * pair
        add_gram(g_ref, pair, x_ref[:, base : base + B], x_ref[:, base + B : base + 2 * B])


def gram_first(x):
    rows = x.shape[0]
    tile = min(TILE, rows)
    return pl.pallas_call(
        gram_first_kernel,
        grid=(rows // tile,),
        in_specs=[pl.BlockSpec((tile, 4 * B), lambda i: (i, 0))],
        out_specs=pl.BlockSpec((2, GROWS, B), lambda i: (0, 0, 0)),
        out_shape=jax.ShapeDtypeStruct((2, GROWS, B), F32),
        compiler_params=PARAMS,
        name="gram_first",
    )(x)


def gram_next_kernel(rebuild, flag_ref, first_ref, last_ref, b0_ref, t1_ref, in_top_ref, in_bottom_ref, *rest):
    if rebuild:
        prev_left_ref, prev_right_ref, q_top_ref, q_bottom_ref, g_in_ref, g_ref, t0_ref, b1_ref = rest
    else:
        g_in_ref, g_ref, t0_ref, b1_ref = rest

    @pl.when(pl.program_id(0) == 0)
    def _():
        g_ref[...] = g_in_ref[...]

    in_top, in_bottom = in_top_ref[...], in_bottom_ref[...]
    if rebuild:
        in_top = dot3(halves(beside(in_top, prev_left_ref[...])), halves(q_top_ref[...]))
        in_bottom = dot3(halves(beside(prev_right_ref[...], in_bottom)), halves(q_bottom_ref[...]))
    t0 = jnp.where(flag_ref[0] == 1, first_ref[...], in_top)
    b1 = jnp.where(flag_ref[1] == 1, last_ref[...], in_bottom)
    t0_ref[...] = t0
    b1_ref[...] = b1
    add_gram(g_ref, 0, t0, b0_ref[...])
    add_gram(g_ref, 1, t1_ref[...], b1)


def gram_next(flags, blocks, rebuilt, g_in):
    rows = blocks[0].shape[0]
    tile = min(TILE, rows)
    block = pl.BlockSpec((tile, B), lambda i: (i, 0))
    half = pl.BlockSpec((2 * B, B), lambda i: (0, 0))
    gram = pl.BlockSpec((2, GROWS, B), lambda i: (0, 0, 0))
    extra = [block, block, half, half] if rebuilt else []
    return pl.pallas_call(
        functools.partial(gram_next_kernel, bool(rebuilt)),
        grid=(rows // tile,),
        in_specs=[pl.BlockSpec(memory_space=pltpu.SMEM)] + [block] * 6 + extra + [gram],
        out_specs=[gram, block, block],
        out_shape=[jax.ShapeDtypeStruct((2, GROWS, B), F32)] + [jax.ShapeDtypeStruct((rows, B), F32)] * 2,
        compiler_params=PARAMS,
        name="gram_next",
    )(flags, *blocks, *rebuilt, g_in)


def polar_kernel(*refs):
    *g_refs, q_ref, right_ref, left_ref = refs
    total = g_refs[0][...]
    for g_ref in g_refs[1:]:
        total = total + g_ref[...]
    eye = (lax.broadcasted_iota(jnp.int32, (B, B), 0) == lax.broadcasted_iota(jnp.int32, (B, B), 1)).astype(F32)
    chains = []
    for pair in range(2):
        gram = total[pair, :B]
        norm_top = jnp.transpose(jnp.broadcast_to(total[pair, B : B + 1], (B, B)))
        norm_bottom = jnp.broadcast_to(total[pair, B + 1 : B + 2], (B, B))
        differ = norm_top - norm_bottom
        both = norm_top + norm_bottom + EPS
        radius = jnp.sqrt(differ * differ + 4.0 * gram * gram)
        denominator = differ * differ + jnp.abs(differ) * radius + DAMPING * both * both
        coupling = -2.0 * gram * differ / denominator
        scale = lax.rsqrt(1.0 + jnp.sum(coupling * coupling, keepdims=True))
        chains.append(beside(eye, coupling) * scale)
        chains.append(beside(-jnp.transpose(coupling), eye) * scale)

    def iterate(_, chains):
        parts = [halves(chain) for chain in chains]
        inner = [halves(dot3(part, part, NT)) for part in parts]
        return tuple(1.5 * chain - 0.5 * dot3(m, part) for chain, m, part in zip(chains, inner, parts))

    chains = lax.fori_loop(0, ITERS, iterate, tuple(chains))
    for pair in range(2):
        q_ref[pair, :B, :] = chains[2 * pair]
        q_ref[pair, B:, :] = chains[2 * pair + 1]
    right_ref[:B, :] = chains[2][:, :B]
    right_ref[B:, :] = chains[3][:, :B]
    left_ref[:B, :] = chains[0][:, B:]
    left_ref[B:, :] = chains[1][:, B:]


def polar(grams):
    return pl.pallas_call(
        polar_kernel,
        out_shape=[
            jax.ShapeDtypeStruct((2, 2 * B, 2 * B), F32),
            jax.ShapeDtypeStruct((2 * B, B), F32),
            jax.ShapeDtypeStruct((2 * B, B), F32),
        ],
        compiler_params=PARAMS,
        name="polar",
    )(*grams)


def rotate_kernel(whole, last, flag_ref, *refs):
    if whole:
        x_ref, q_ref, *outs = refs
        pairs = [x_ref[:, : 2 * B], x_ref[:, 2 * B :]]
    else:
        t0_ref, b0_ref, t1_ref, b1_ref, q_ref, *outs = refs
        pairs = [beside(t0_ref[...], b0_ref[...]), beside(t1_ref[...], b1_ref[...])]
    turned = [dot3(halves(pairs[k]), halves(q_ref[k])) for k in range(2)]
    if last:
        outs[0][:, : 2 * B] = turned[0]
        outs[0][:, 2 * B :] = turned[1]
        return
    right_ref, left_ref, t1n_ref, b0n_ref = outs
    first = flag_ref[0] == 1
    t0, b0 = turned[0][:, :B], turned[0][:, B:]
    right_ref[...] = turned[1][:, :B]
    left_ref[...] = jnp.where(first, t0, b0)
    t1n_ref[...] = jnp.where(first, b0, t0)
    b0n_ref[...] = turned[1][:, B:]


def rotate(flags, blocks, q, last=False, rows=None, start=0):
    whole = len(blocks) == 1
    rows = rows or blocks[0].shape[0]
    tile = min(TILE, rows)
    offset = start // tile
    block = pl.BlockSpec((tile, B), lambda i: (i, 0))
    wide = pl.BlockSpec((tile, 4 * B), lambda i: (i + offset, 0))
    full = pl.BlockSpec((2, 2 * B, 2 * B), lambda i: (0, 0, 0))
    if last:
        out_specs, out_shape = wide, jax.ShapeDtypeStruct((rows, 4 * B), F32)
    else:
        out_specs, out_shape = [block] * 4, [jax.ShapeDtypeStruct((rows, B), F32)] * 4
    return pl.pallas_call(
        functools.partial(rotate_kernel, whole, last),
        grid=(rows // tile,),
        in_specs=[pl.BlockSpec(memory_space=pltpu.SMEM)] + ([wide] if whole else [block] * 4) + [full],
        out_specs=out_specs,
        out_shape=out_shape,
        compiler_params=PARAMS,
        name="rotate",
    )(flags, *blocks, q)


def shifted(value, steps):
    count = lax.axis_size("pair")
    initial, last = (max(0, -steps), min(count, count - steps))
    return lax.ppermute(value, "pair", [(source, source + steps) for source in range(initial, last)])


def row_terms(g, relayed):
    rows, pairs = lax.axis_size("row"), lax.axis_size("pair")
    part = g + lax.ppermute(g, "row", [(r, r ^ 1) for r in range(rows)])
    if not relayed:
        return [part, lax.ppermute(part, "row", [(r, r ^ 2) for r in range(rows)])]
    both = ("pair", "row")
    relay = {0: RELAY, pairs - 1: pairs - 1 - RELAY}
    here = [p * rows + r for p in range(pairs) if p not in relay for r in range(rows)]
    ends = [(p * rows + r, via * rows + r) for p, via in relay.items() for r in range(rows)]
    hop = lax.ppermute(part, both, [(end, via ^ 2) for end, via in ends])
    direct = lax.ppermute(part, both, [(i, i ^ 2) for i in here])
    return [part, direct, lax.ppermute(hop, both, [(via, end) for end, via in ends])]


def after(values, done):
    return lax.optimization_barrier((values, done))


def per_device(factor):
    position = lax.axis_index("pair")
    flags = jnp.stack([position == 0, position == lax.axis_size("pair") - 1]).astype(jnp.int32)
    zero = jnp.zeros((2, GROWS, B), F32)

    q, _, _ = polar(row_terms(gram_first(factor), False))
    right, left, t1, b0 = rotate(flags, [factor], q)
    arrived = (shifted(right, 1), shifted(left, -1))
    (t1, b0), arrived = after((t1, b0), arrived)
    ahead = (shifted(t1, 1), shifted(b0, -1))
    previous = (left, right)
    rebuilt = ()
    for step in range(1, STEPS):
        g, t0, b1 = gram_next(flags, (left, right, b0, t1, *arrived), rebuilt, zero)
        q, q_right, q_left = polar(row_terms(g, step < STEPS - 1))
        if step == STEPS - 1:
            return rotate(flags, [t0, b0, t1, b1], q, last=True)
        q_top, q_bottom = shifted(q_right, 1), shifted(q_left, -1)
        older = previous
        right, left, t1, b0 = rotate(flags, [t0, b0, t1, b1], q)
        previous = (left, right)
        rebuilt = (*older, q_top, q_bottom)
        arrived = ahead
        if step < STEPS - 2:
            (t1, b0), (arrived, rebuilt) = after((t1, b0), (arrived, rebuilt))
            ahead = (shifted(t1, 1), shifted(b0, -1))


def solution(mesh):
    placed = (P("row", "pair"),)
    return jax.shard_map(
        per_device, mesh=mesh, in_specs=placed, out_specs=P("row", "pair"), check_vma=False
    )
```

```python
import functools
import jax
import jax.numpy as jnp
from jax import lax
from jax.experimental import pallas as pl
from jax.experimental.pallas import tpu as pltpu
from jax.sharding import PartitionSpec as P

B = 128
STEPS = 4
ITERS = 12
EPS = 1e-06
DAMPING = 0.04
TILE = 1024
GROWS = 136
RELAY = 5
F32 = jnp.float32
BF16 = jnp.bfloat16
PARAMS = pltpu.CompilerParams(vmem_limit_bytes=24 * 1024 * 1024)
NN = (((1,), (0,)), ((), ()))
NT = (((1,), (1,)), ((), ()))
TN = (((0,), (0,)), ((), ()))


def halves(value):
    high = value.astype(BF16)
    return high, (value - high.astype(F32)).astype(BF16)


def dot(a, b, dims=NN):
    return lax.dot_general(a, b, dims, preferred_element_type=F32)


def dot3(a, b, dims=NN):
    return dot(a[0], b[0], dims) + (dot(a[0], b[1], dims) + dot(a[1], b[0], dims))


def beside(a, b):
    return jnp.concatenate([a, b], axis=1)


def dot3_narrow(a, b):
    y = dot(a[0], beside(*b))
    return (y[:, :B] + y[:, B:]) + dot(a[1], b[0])


def add_gram(g_ref, pair, top, bottom):
    product = dot(beside(*halves(top)), beside(*halves(bottom)), TN)
    g_ref[pair, :B, :] += (product[:B, :B] + product[B:, B:]) + (product[:B, B:] + product[B:, :B])
    g_ref[pair, B : B + 1, :] += jnp.sum(top * top, axis=0, keepdims=True)
    g_ref[pair, B + 1 : B + 2, :] += jnp.sum(bottom * bottom, axis=0, keepdims=True)


def gram_first_kernel(x_ref, g_ref):
    @pl.when(pl.program_id(0) == 0)
    def _():
        g_ref[...] = jnp.zeros_like(g_ref)

    for pair in range(2):
        base = 2 * B * pair
        add_gram(g_ref, pair, x_ref[:, base : base + B], x_ref[:, base + B : base + 2 * B])


def gram_first(x):
    rows = x.shape[0]
    tile = min(TILE, rows)
    return pl.pallas_call(
        gram_first_kernel,
        grid=(rows // tile,),
        in_specs=[pl.BlockSpec((tile, 4 * B), lambda i: (i, 0))],
        out_specs=pl.BlockSpec((2, GROWS, B), lambda i: (0, 0, 0)),
        out_shape=jax.ShapeDtypeStruct((2, GROWS, B), F32),
        compiler_params=PARAMS,
        name="gram_first",
    )(x)


def gram_next_kernel(rebuild, flag_ref, first_ref, last_ref, b0_ref, t1_ref, in_top_ref, in_bottom_ref, *rest):
    if rebuild:
        prev_left_ref, prev_right_ref, q_top_ref, q_bottom_ref, g_in_ref, g_ref, t0_ref, b1_ref = rest
    else:
        g_in_ref, g_ref, t0_ref, b1_ref = rest

    @pl.when(pl.program_id(0) == 0)
    def _():
        g_ref[...] = g_in_ref[...]

    in_top, in_bottom = in_top_ref[...], in_bottom_ref[...]
    if rebuild:
        in_top = dot3_narrow(halves(beside(in_top, prev_left_ref[...])), halves(q_top_ref[...]))
        in_bottom = dot3_narrow(halves(beside(prev_right_ref[...], in_bottom)), halves(q_bottom_ref[...]))
    t0 = jnp.where(flag_ref[0] == 1, first_ref[...], in_top)
    b1 = jnp.where(flag_ref[1] == 1, last_ref[...], in_bottom)
    t0_ref[...] = t0
    b1_ref[...] = b1
    add_gram(g_ref, 0, t0, b0_ref[...])
    add_gram(g_ref, 1, t1_ref[...], b1)


def gram_next(flags, blocks, rebuilt, g_in):
    rows = blocks[0].shape[0]
    tile = min(TILE, rows)
    block = pl.BlockSpec((tile, B), lambda i: (i, 0))
    half = pl.BlockSpec((2 * B, B), lambda i: (0, 0))
    gram = pl.BlockSpec((2, GROWS, B), lambda i: (0, 0, 0))
    extra = [block, block, half, half] if rebuilt else []
    return pl.pallas_call(
        functools.partial(gram_next_kernel, bool(rebuilt)),
        grid=(rows // tile,),
        in_specs=[pl.BlockSpec(memory_space=pltpu.SMEM)] + [block] * 6 + extra + [gram],
        out_specs=[gram, block, block],
        out_shape=[jax.ShapeDtypeStruct((2, GROWS, B), F32)] + [jax.ShapeDtypeStruct((rows, B), F32)] * 2,
        compiler_params=PARAMS,
        name="gram_next",
    )(flags, *blocks, *rebuilt, g_in)


def polar_kernel(swap, flag_ref, *refs):
    *g_refs, q_ref, right_ref, left_ref = refs
    total = g_refs[0][...]
    for g_ref in g_refs[1:]:
        total = total + g_ref[...]
    eye = (lax.broadcasted_iota(jnp.int32, (B, B), 0) == lax.broadcasted_iota(jnp.int32, (B, B), 1)).astype(F32)
    chains = []
    for pair in range(2):
        gram = total[pair, :B]
        norm_top = jnp.transpose(jnp.broadcast_to(total[pair, B : B + 1], (B, B)))
        norm_bottom = jnp.broadcast_to(total[pair, B + 1 : B + 2], (B, B))
        differ = norm_top - norm_bottom
        both = norm_top + norm_bottom + EPS
        radius = jnp.sqrt(differ * differ + 4.0 * gram * gram)
        denominator = differ * differ + jnp.abs(differ) * radius + DAMPING * both * both
        coupling = -2.0 * gram * differ / denominator
        scale = lax.rsqrt(1.0 + jnp.sum(coupling * coupling, keepdims=True))
        chains.append(beside(eye, coupling) * scale)
        chains.append(beside(-jnp.transpose(coupling), eye) * scale)

    def iterate(_, chains):
        parts = [halves(chain) for chain in chains]
        inner = [halves(dot3(part, part, NT)) for part in parts]
        return tuple(1.5 * chain - 0.5 * dot3(m, part) for chain, m, part in zip(chains, inner, parts))

    chains = lax.fori_loop(0, ITERS, iterate, tuple(chains), unroll=ITERS)
    for half in range(2):
        rows = pl.ds(half * B, B)
        top, bottom = chains[half][:, :B], chains[half][:, B:]
        left_ref[rows, :] = bottom
        if swap:
            first = flag_ref[0] == 1
            top, bottom = jnp.where(first, bottom, top), jnp.where(first, top, bottom)
        q_ref[0, rows, :] = beside(top, bottom)
        q_ref[1, rows, :] = chains[2 + half]
        right_ref[rows, :] = chains[2 + half][:, :B]


def polar(flags, grams, swap=True):
    return pl.pallas_call(
        functools.partial(polar_kernel, swap),
        in_specs=[pl.BlockSpec(memory_space=pltpu.SMEM)] + [pl.BlockSpec(memory_space=pltpu.VMEM)] * len(grams),
        out_shape=[
            jax.ShapeDtypeStruct((2, 2 * B, 2 * B), F32),
            jax.ShapeDtypeStruct((2 * B, B), F32),
            jax.ShapeDtypeStruct((2 * B, B), F32),
        ],
        compiler_params=PARAMS,
        name="polar",
    )(flags, *grams)


def rotate_kernel(t0_ref, b0_ref, t1_ref, b1_ref, q_ref, *outs):
    for pair, (top_ref, bottom_ref) in enumerate(((t0_ref, b0_ref), (t1_ref, b1_ref))):
        turned = dot3(halves(beside(top_ref[...], bottom_ref[...])), halves(q_ref[pair]))
        if len(outs) == 1:
            outs[0][:, 2 * B * pair : 2 * B * (pair + 1)] = turned
        else:
            outs[2 * pair][...] = turned[:, :B]
            outs[2 * pair + 1][...] = turned[:, B:]


def rotate(blocks, q, last=False):
    rows = blocks[0].shape[0]
    tile = min(TILE, rows)
    block = pl.BlockSpec((tile, B), lambda i: (i, 0))
    full = pl.BlockSpec((2, 2 * B, 2 * B), lambda i: (0, 0, 0))
    if last:
        out_specs, out_shape = pl.BlockSpec((tile, 4 * B), lambda i: (i, 0)), jax.ShapeDtypeStruct((rows, 4 * B), F32)
    else:
        out_specs, out_shape = [block] * 4, [jax.ShapeDtypeStruct((rows, B), F32)] * 4
    return pl.pallas_call(
        rotate_kernel,
        grid=(rows // tile,),
        in_specs=[block] * 4 + [full],
        out_specs=out_specs,
        out_shape=out_shape,
        compiler_params=PARAMS,
        name="rotate",
    )(*blocks, q)


def rotate_part_kernel(columns, x_ref, q_ref, *outs):
    for pair in range(2):
        q = halves(q_ref[pair, :, columns[pair] : columns[pair] + B])
        outs[pair][...] = dot3_narrow(halves(x_ref[:, 2 * B * pair : 2 * B * (pair + 1)]), q)


def rotate_part(x, q, columns):
    rows = x.shape[0]
    tile = min(TILE, rows)
    block = pl.BlockSpec((tile, B), lambda i: (i, 0))
    return pl.pallas_call(
        functools.partial(rotate_part_kernel, columns),
        grid=(rows // tile,),
        in_specs=[pl.BlockSpec((tile, 4 * B), lambda i: (i, 0)), pl.BlockSpec((2, 2 * B, 2 * B), lambda i: (0, 0, 0))],
        out_specs=[block] * 2,
        out_shape=[jax.ShapeDtypeStruct((rows, B), F32)] * 2,
        compiler_params=PARAMS,
        name="rotate_part",
    )(x, q)


def shifted(value, steps):
    count = lax.axis_size("pair")
    initial, last = (max(0, -steps), min(count, count - steps))
    return lax.ppermute(value, "pair", [(source, source + steps) for source in range(initial, last)])


def row_terms(g, relayed):
    rows, pairs = lax.axis_size("row"), lax.axis_size("pair")
    part = g + lax.ppermute(g, "row", [(r, r ^ 1) for r in range(rows)])
    if not relayed:
        return [part, lax.ppermute(part, "row", [(r, r ^ 2) for r in range(rows)])]
    both = ("pair", "row")
    relay = {0: RELAY, pairs - 1: pairs - 1 - RELAY}
    here = [p * rows + r for p in range(pairs) if p not in relay for r in range(rows)]
    ends = [(p * rows + r, via * rows + r) for p, via in relay.items() for r in range(rows)]
    hop = lax.ppermute(part, both, [(end, via ^ 2) for end, via in ends])
    direct = lax.ppermute(part, both, [(i, i ^ 2) for i in here])
    return [part, direct, lax.ppermute(hop, both, [(via, end) for end, via in ends])]


def after(values, done):
    return lax.optimization_barrier((values, done))


def per_device(factor):
    position = lax.axis_index("pair")
    flags = jnp.stack([position == 0, position == lax.axis_size("pair") - 1]).astype(jnp.int32)
    zero = jnp.zeros((2, GROWS, B), F32)

    q, _, _ = polar(flags, row_terms(gram_first(factor), False))
    left, right = rotate_part(factor, q, (B, 0))
    arrived = (shifted(right, 1), shifted(left, -1))
    t1, b0 = rotate_part(factor, q, (0, B))
    (t1, b0), arrived = after((t1, b0), arrived)
    ahead = (shifted(t1, 1), shifted(b0, -1))
    previous = (left, right)
    rebuilt = ()
    for step in range(1, STEPS):
        g, t0, b1 = gram_next(flags, (left, right, b0, t1, *arrived), rebuilt, zero)
        q, q_right, q_left = polar(flags, row_terms(g, step < STEPS - 1), step < STEPS - 1)
        if step == STEPS - 1:
            return rotate([t0, b0, t1, b1], q, last=True)
        q_top, q_bottom = shifted(q_right, 1), shifted(q_left, -1)
        older = previous
        t1, left, right, b0 = rotate([t0, b0, t1, b1], q)
        previous = (left, right)
        rebuilt = (*older, q_top, q_bottom)
        arrived = ahead
        if step < STEPS - 2:
            (t1, b0), (arrived, rebuilt) = after((t1, b0), (arrived, rebuilt))
            ahead = (shifted(t1, 1), shifted(b0, -1))


def solution(mesh):
    placed = (P("row", "pair"),)
    return jax.shard_map(
        per_device, mesh=mesh, in_specs=placed, out_specs=P("row", "pair"), check_vma=False
    )
```

```python
import functools
import jax
import jax.numpy as jnp
from jax import lax
from jax.experimental import pallas as pl
from jax.experimental.pallas import tpu as pltpu
from jax.sharding import PartitionSpec as P

B = 128
STEPS = 4
ITERS = 12
EPS = 1e-06
DAMPING = 0.04
TILE = 1024
GROWS = 136
LOADS = 4
RELAY = 5
F32 = jnp.float32
BF16 = jnp.bfloat16
LONG = pl.CostEstimate(flops=60 * 10**9, bytes_accessed=1 << 20, transcendentals=0)
SHORT = pl.CostEstimate(flops=5 * 10**9, bytes_accessed=1 << 20, transcendentals=0)
PARAMS = pltpu.CompilerParams(vmem_limit_bytes=20 * 1024 * 1024)
NN = (((1,), (0,)), ((), ()))
NT = (((1,), (1,)), ((), ()))
TN = (((0,), (0,)), ((), ()))


def halves(value):
    high = value.astype(BF16)
    return high, (value - high.astype(F32)).astype(BF16)


def dot(a, b, dims=NN):
    return lax.dot_general(a, b, dims, preferred_element_type=F32)


def dot3(a, b, dims=NN):
    return dot(a[0], b[0], dims) + (dot(a[0], b[1], dims) + dot(a[1], b[0], dims))


def beside(a, b):
    return jnp.concatenate([a, b], axis=1)


def dot3_narrow(a, b):
    y = dot(a[0], beside(*b))
    return (y[:, :B] + y[:, B:]) + dot(a[1], b[0])


def add_gram(g_ref, pair, top, bottom):
    product = dot(beside(*halves(top)), beside(*halves(bottom)), TN)
    g_ref[pair, :B, :] += (product[:B, :B] + product[B:, B:]) + (product[:B, B:] + product[B:, :B])
    g_ref[pair, B : B + 1, :] += jnp.sum(top * top, axis=0, keepdims=True)
    g_ref[pair, B + 1 : B + 2, :] += jnp.sum(bottom * bottom, axis=0, keepdims=True)


def gram_first_kernel(x_ref, copy_ref, g_ref, sems):
    tile = x_ref.shape[0] // LOADS
    loads = []
    for i in range(LOADS):
        rows = pl.ds(i * tile, tile)
        loads.append(pltpu.make_async_copy(x_ref.at[rows], copy_ref.at[rows], sems.at[i]))
        loads[-1].start()
    g_ref[...] = jnp.zeros_like(g_ref)
    for i in range(LOADS):
        loads[i].wait()
        for pair in range(2):
            base = 2 * B * pair
            rows = slice(i * tile, (i + 1) * tile)
            add_gram(g_ref, pair, copy_ref[rows, base : base + B], copy_ref[rows, base + B : base + 2 * B])


def gram_first(x):
    vmem = pl.BlockSpec(memory_space=pltpu.VMEM)
    return pl.pallas_call(
        gram_first_kernel,
        in_specs=[pl.BlockSpec(memory_space=pl.ANY)],
        out_specs=[vmem, vmem],
        out_shape=[jax.ShapeDtypeStruct(x.shape, F32), jax.ShapeDtypeStruct((2, GROWS, B), F32)],
        scratch_shapes=[pltpu.SemaphoreType.DMA((LOADS,))],
        compiler_params=pltpu.CompilerParams(vmem_limit_bytes=40 * 1024 * 1024),
        name="gram_first",
    )(x)


def gram_next_kernel(rebuild, flag_ref, first_ref, last_ref, b0_ref, t1_ref, in_top_ref, in_bottom_ref, *rest):
    if rebuild:
        prev_left_ref, prev_right_ref, q_top_ref, q_bottom_ref, g_in_ref, g_ref, t0_ref, b1_ref = rest
    else:
        g_in_ref, g_ref, t0_ref, b1_ref = rest

    @pl.when(pl.program_id(0) == 0)
    def _():
        g_ref[...] = g_in_ref[...]

    in_top, in_bottom = in_top_ref[...], in_bottom_ref[...]
    if rebuild:
        in_top = dot3_narrow(halves(beside(in_top, prev_left_ref[...])), halves(q_top_ref[...]))
        in_bottom = dot3_narrow(halves(beside(prev_right_ref[...], in_bottom)), halves(q_bottom_ref[...]))
    t0 = jnp.where(flag_ref[0] == 1, first_ref[...], in_top)
    b1 = jnp.where(flag_ref[1] == 1, last_ref[...], in_bottom)
    t0_ref[...] = t0
    b1_ref[...] = b1
    add_gram(g_ref, 0, t0, b0_ref[...])
    add_gram(g_ref, 1, t1_ref[...], b1)


def gram_next(flags, blocks, rebuilt, g_in):
    rows = blocks[0].shape[0]
    tile = min(TILE, rows)
    block = pl.BlockSpec((tile, B), lambda i: (i, 0))
    half = pl.BlockSpec((2 * B, B), lambda i: (0, 0))
    gram = pl.BlockSpec((2, GROWS, B), lambda i: (0, 0, 0))
    extra = [block, block, half, half] if rebuilt else []
    return pl.pallas_call(
        functools.partial(gram_next_kernel, bool(rebuilt)),
        grid=(rows // tile,),
        in_specs=[pl.BlockSpec(memory_space=pltpu.SMEM)] + [block] * 6 + extra + [gram],
        out_specs=[gram, block, block],
        out_shape=[jax.ShapeDtypeStruct((2, GROWS, B), F32)] + [jax.ShapeDtypeStruct((rows, B), F32)] * 2,
        compiler_params=PARAMS,
        cost_estimate=LONG,
        name="gram_next",
    )(flags, *blocks, *rebuilt, g_in)


def polar_kernel(swap, flag_ref, *refs):
    *g_refs, q_ref, right_ref, left_ref = refs
    total = g_refs[0][...]
    for g_ref in g_refs[1:]:
        total = total + g_ref[...]
    eye = (lax.broadcasted_iota(jnp.int32, (B, B), 0) == lax.broadcasted_iota(jnp.int32, (B, B), 1)).astype(F32)
    chains = []
    for pair in range(2):
        gram = total[pair, :B]
        norm_top = jnp.transpose(jnp.broadcast_to(total[pair, B : B + 1], (B, B)))
        norm_bottom = jnp.broadcast_to(total[pair, B + 1 : B + 2], (B, B))
        differ = norm_top - norm_bottom
        both = norm_top + norm_bottom + EPS
        radius = jnp.sqrt(differ * differ + 4.0 * gram * gram)
        denominator = differ * differ + jnp.abs(differ) * radius + DAMPING * both * both
        coupling = -2.0 * gram * differ / denominator
        scale = lax.rsqrt(1.0 + jnp.sum(coupling * coupling, keepdims=True))
        chains.append(beside(eye, coupling) * scale)
        chains.append(beside(-jnp.transpose(coupling), eye) * scale)

    def iterate(_, chains):
        parts = [halves(chain) for chain in chains]
        inner = [halves(dot3(part, part, NT)) for part in parts]
        return tuple(1.5 * chain - 0.5 * dot3(m, part) for chain, m, part in zip(chains, inner, parts))

    chains = lax.fori_loop(0, ITERS, iterate, tuple(chains), unroll=ITERS)
    for half in range(2):
        rows = pl.ds(half * B, B)
        top, bottom = chains[half][:, :B], chains[half][:, B:]
        left_ref[rows, :] = bottom
        if swap:
            first = flag_ref[0] == 1
            top, bottom = jnp.where(first, bottom, top), jnp.where(first, top, bottom)
        q_ref[0, rows, :] = beside(top, bottom)
        q_ref[1, rows, :] = chains[2 + half]
        right_ref[rows, :] = chains[2 + half][:, :B]


def polar(flags, grams, swap=True):
    return pl.pallas_call(
        functools.partial(polar_kernel, swap),
        in_specs=[pl.BlockSpec(memory_space=pltpu.SMEM)] + [pl.BlockSpec(memory_space=pltpu.VMEM)] * len(grams),
        out_shape=[
            jax.ShapeDtypeStruct((2, 2 * B, 2 * B), F32),
            jax.ShapeDtypeStruct((2 * B, B), F32),
            jax.ShapeDtypeStruct((2 * B, B), F32),
        ],
        compiler_params=PARAMS,
        cost_estimate=SHORT,
        name="polar",
    )(flags, *grams)


def rotate_kernel(t0_ref, b0_ref, t1_ref, b1_ref, q_ref, *outs):
    for pair, (top_ref, bottom_ref) in enumerate(((t0_ref, b0_ref), (t1_ref, b1_ref))):
        turned = dot3(halves(beside(top_ref[...], bottom_ref[...])), halves(q_ref[pair]))
        if len(outs) == 1:
            outs[0][:, 2 * B * pair : 2 * B * (pair + 1)] = turned
        else:
            outs[2 * pair][...] = turned[:, :B]
            outs[2 * pair + 1][...] = turned[:, B:]


def rotate(blocks, q, last=False):
    rows = blocks[0].shape[0]
    tile = min(TILE, rows)
    block = pl.BlockSpec((tile, B), lambda i: (i, 0))
    full = pl.BlockSpec((2, 2 * B, 2 * B), lambda i: (0, 0, 0))
    if last:
        out_specs, out_shape = pl.BlockSpec((tile, 4 * B), lambda i: (i, 0)), jax.ShapeDtypeStruct((rows, 4 * B), F32)
    else:
        out_specs, out_shape = [block] * 4, [jax.ShapeDtypeStruct((rows, B), F32)] * 4
    return pl.pallas_call(
        rotate_kernel,
        grid=(rows // tile,),
        in_specs=[block] * 4 + [full],
        out_specs=out_specs,
        out_shape=out_shape,
        compiler_params=PARAMS,
        cost_estimate=SHORT,
        name="rotate",
    )(*blocks, q)


def rotate_part_kernel(columns, x_ref, q_ref, *outs):
    for pair in range(2):
        q = halves(q_ref[pair, :, columns[pair] : columns[pair] + B])
        outs[pair][...] = dot3_narrow(halves(x_ref[:, 2 * B * pair : 2 * B * (pair + 1)]), q)


def rotate_part(x, q, columns):
    rows = x.shape[0]
    tile = min(TILE, rows)
    block = pl.BlockSpec((tile, B), lambda i: (i, 0))
    return pl.pallas_call(
        functools.partial(rotate_part_kernel, columns),
        grid=(rows // tile,),
        in_specs=[pl.BlockSpec((tile, 4 * B), lambda i: (i, 0)), pl.BlockSpec((2, 2 * B, 2 * B), lambda i: (0, 0, 0))],
        out_specs=[block] * 2,
        out_shape=[jax.ShapeDtypeStruct((rows, B), F32)] * 2,
        compiler_params=PARAMS,
        name="rotate_part",
    )(x, q)


def shifted(value, steps):
    count = lax.axis_size("pair")
    initial, last = (max(0, -steps), min(count, count - steps))
    return lax.ppermute(value, "pair", [(source, source + steps) for source in range(initial, last)])


def row_terms(g, relayed):
    rows, pairs = lax.axis_size("row"), lax.axis_size("pair")
    part = g + lax.ppermute(g, "row", [(r, r ^ 1) for r in range(rows)])
    if not relayed:
        return [part, lax.ppermute(part, "row", [(r, r ^ 2) for r in range(rows)])]
    both = ("pair", "row")
    relay = {0: RELAY, pairs - 1: pairs - 1 - RELAY}
    here = [p * rows + r for p in range(pairs) if p not in relay for r in range(rows)]
    ends = [(p * rows + r, via * rows + r) for p, via in relay.items() for r in range(rows)]
    hop = lax.ppermute(part, both, [(end, via ^ 2) for end, via in ends])
    direct = lax.ppermute(part, both, [(i, i ^ 2) for i in here])
    return [part, direct, lax.ppermute(hop, both, [(via, end) for end, via in ends])]


def per_device(factor):
    position = lax.axis_index("pair")
    flags = jnp.stack([position == 0, position == lax.axis_size("pair") - 1]).astype(jnp.int32)
    zero = jnp.zeros((2, GROWS, B), F32)

    factor, g = gram_first(factor)
    q, _, _ = polar(flags, row_terms(g, False))
    left, right = rotate_part(factor, q, (B, 0))
    arrived = (shifted(right, 1), shifted(left, -1))
    t1, b0 = rotate_part(factor, q, (0, B))
    ahead = (shifted(t1, 1), shifted(b0, -1))
    previous = (left, right)
    rebuilt = ()
    for step in range(1, STEPS):
        g, t0, b1 = gram_next(flags, (left, right, b0, t1, *arrived), rebuilt, zero)
        q, q_right, q_left = polar(flags, row_terms(g, step < STEPS - 1), step < STEPS - 1)
        if step == STEPS - 1:
            return rotate([t0, b0, t1, b1], q, last=True)
        q_top, q_bottom = shifted(q_right, 1), shifted(q_left, -1)
        rebuilt = (*previous, q_top, q_bottom)
        t1, left, right, b0 = rotate([t0, b0, t1, b1], q)
        previous = (left, right)
        arrived = ahead
        if step < STEPS - 2:
            ahead = (shifted(t1, 1), shifted(b0, -1))


def solution(mesh):
    placed = (P("row", "pair"),)
    return jax.shard_map(
        per_device, mesh=mesh, in_specs=placed, out_specs=P("row", "pair"), check_vma=False
    )
```

```python
import functools
import jax
import jax.numpy as jnp
from jax import lax
from jax.experimental import pallas as pl
from jax.experimental.pallas import tpu as pltpu
from jax.sharding import PartitionSpec as P

B = 128
ITERS = 12
EPS = 1e-06
DAMPING = 0.04
TILE = 1024
GROWS = 136
LOADS = 4
LATE = 512
RELAY = 5
F32 = jnp.float32
BF16 = jnp.bfloat16
LONG = pl.CostEstimate(flops=60 * 10**9, bytes_accessed=1 << 20, transcendentals=0)
SHORT = pl.CostEstimate(flops=5 * 10**9, bytes_accessed=1 << 20, transcendentals=0)
NONE = pl.CostEstimate(flops=10**6, bytes_accessed=1 << 10, transcendentals=0)
MIB = 1024 * 1024
PARAMS = pltpu.CompilerParams(vmem_limit_bytes=20 * MIB)
NN = (((1,), (0,)), ((), ()))
NT = (((1,), (1,)), ((), ()))
TN = (((0,), (0,)), ((), ()))
VMEM = pl.BlockSpec(memory_space=pltpu.VMEM)
ANY = pl.BlockSpec(memory_space=pl.ANY)
SMEM = pl.BlockSpec(memory_space=pltpu.SMEM)


def halves(value):
    high = value.astype(BF16)
    return high, (value - high.astype(F32)).astype(BF16)


def dot(a, b, dims=NN):
    return lax.dot_general(a, b, dims, preferred_element_type=F32)


def dot3(a, b, dims=NN):
    return dot(a[0], b[0], dims) + (dot(a[0], b[1], dims) + dot(a[1], b[0], dims))


def beside(a, b):
    return jnp.concatenate([a, b], axis=1)


def thirds(value):
    high = value.astype(BF16)
    rest = value - high.astype(F32)
    middle = rest.astype(BF16)
    return high, middle, (rest - middle.astype(F32)).astype(BF16)


def dot4(a, b):
    return dot(a[0], b[0]) + ((dot(a[0], b[1]) + dot(a[1], b[0])) + dot(a[0], b[2]))


def dot4_narrow(a, b):
    y = dot(a[0], beside(b[0], b[1]))
    return y[:, :B] + (y[:, B:] + (dot(a[1], b[0]) + dot(a[0], b[2])))


def add_gram(g_ref, pair, top, bottom):
    product = dot(beside(*halves(top)), beside(*halves(bottom)), TN)
    g_ref[pair, :B, :] += (product[:B, :B] + product[B:, B:]) + (product[:B, B:] + product[B:, :B])
    g_ref[pair, B : B + 1, :] += jnp.sum(top * top, axis=0, keepdims=True)
    g_ref[pair, B + 1 : B + 2, :] += jnp.sum(bottom * bottom, axis=0, keepdims=True)


def gram_first_kernel(x_ref, g_ref, copy_ref, sems):
    tile = x_ref.shape[0] // LOADS
    loads = []
    for i in range(LOADS):
        rows = pl.ds(i * tile, tile)
        loads.append(pltpu.make_async_copy(x_ref.at[rows], copy_ref.at[rows], sems.at[i]))
        loads[-1].start()
    g_ref[...] = jnp.zeros_like(g_ref)
    for i in range(LOADS):
        loads[i].wait()
        for pair in range(2):
            base = 2 * B * pair
            rows = slice(i * tile, (i + 1) * tile)
            add_gram(g_ref, pair, copy_ref[rows, base : base + B], copy_ref[rows, base + B : base + 2 * B])


def gram_first(x):
    return pl.pallas_call(
        gram_first_kernel,
        in_specs=[ANY],
        out_specs=VMEM,
        out_shape=jax.ShapeDtypeStruct((2, GROWS, B), F32),
        scratch_shapes=[pltpu.VMEM(x.shape, F32), pltpu.SemaphoreType.DMA((LOADS,))],
        compiler_params=pltpu.CompilerParams(vmem_limit_bytes=56 * MIB),
        name="gram_first",
    )(x)


def gram_next_kernel(rebuild, flag_ref, first_ref, last_ref, b0_ref, t1_ref, in_top_ref, in_bottom_ref, *rest):
    if rebuild:
        prev_left_ref, prev_right_ref, own_ref, other_ref, *rest = rest
    g_in_ref, *_, g_ref, t0_ref, b1_ref = rest

    @pl.when(pl.program_id(0) == 0)
    def _():
        g_ref[...] = g_in_ref[...]

    in_top, in_bottom = in_top_ref[...], in_bottom_ref[...]
    if rebuild:
        q_top = jnp.where(flag_ref[2] == 0, own_ref[...], other_ref[...])
        q_bottom = jnp.where(flag_ref[2] == 0, other_ref[...], own_ref[...])
        in_top = dot4_narrow(halves(beside(in_top, prev_left_ref[...])), thirds(q_top))
        in_bottom = dot4_narrow(halves(beside(prev_right_ref[...], in_bottom)), thirds(q_bottom))
    t0 = jnp.where(flag_ref[0] == 1, first_ref[...], in_top)
    b1 = jnp.where(flag_ref[1] == 1, last_ref[...], in_bottom)
    t0_ref[...] = t0
    b1_ref[...] = b1
    add_gram(g_ref, 0, t0, b0_ref[...])
    add_gram(g_ref, 1, t1_ref[...], b1)


def gram_next(flags, blocks, arrived, rebuilt, g_in, start=0, written=()):
    rows, count = blocks[0].shape[0], arrived[0].shape[0]
    tile = max(t for t in (128, 256, 512, 896, 1024) if count % t == 0 and start % t == 0)
    offset = start // tile
    block = pl.BlockSpec((tile, B), lambda i: (i + offset, 0))
    part = pl.BlockSpec((tile, B), lambda i: (i, 0))
    half = pl.BlockSpec((2 * B, B), lambda i: (0, 0))
    gram = pl.BlockSpec((2, GROWS, B), lambda i: (0, 0, 0))
    extra = [block, block, half, half] if rebuilt else []
    in_specs = [SMEM] + [block] * 4 + [part] * 2 + extra + [gram] + [ANY] * len(written)
    return pl.pallas_call(
        functools.partial(gram_next_kernel, bool(rebuilt)),
        grid=(count // tile,),
        in_specs=in_specs,
        out_specs=[gram, block, block],
        out_shape=[jax.ShapeDtypeStruct((2, GROWS, B), F32)] + [jax.ShapeDtypeStruct((rows, B), F32)] * 2,
        input_output_aliases={len(in_specs) - 2 + i: 1 + i for i in range(len(written))},
        compiler_params=PARAMS,
        cost_estimate=LONG if count == rows else NONE,
        name="gram_next",
    )(flags, *blocks, *arrived, *rebuilt, g_in, *written)


def polar_kernel(terms, swap, share, load, flag_ref, *refs):
    g_refs, refs = refs[:terms], refs[terms:]
    if load:
        x_ref, q_ref, copy_ref, sem = refs
        loading = pltpu.make_async_copy(x_ref, copy_ref, sem)
        loading.start()
    else:
        q_ref, *share_refs = refs
    total = g_refs[0][...]
    for g_ref in g_refs[1:]:
        total = total + g_ref[...]
    eye = (lax.broadcasted_iota(jnp.int32, (B, B), 0) == lax.broadcasted_iota(jnp.int32, (B, B), 1)).astype(F32)
    chains = []
    for pair in range(2):
        gram = total[pair, :B]
        norm_top = jnp.transpose(jnp.broadcast_to(total[pair, B : B + 1], (B, B)))
        norm_bottom = jnp.broadcast_to(total[pair, B + 1 : B + 2], (B, B))
        differ = norm_top - norm_bottom
        both = norm_top + norm_bottom + EPS
        radius = jnp.sqrt(differ * differ + 4.0 * gram * gram)
        denominator = differ * differ + jnp.abs(differ) * radius + DAMPING * both * both
        coupling = -2.0 * gram * differ / denominator
        scale = lax.rsqrt(1.0 + jnp.sum(coupling * coupling, keepdims=True))
        chains.append(beside(eye, coupling) * scale)
        chains.append(beside(-jnp.transpose(coupling), eye) * scale)

    def iterate(_, chains):
        parts = [thirds(chain) for chain in chains]
        inner = []
        for h, m, l in parts:
            y = dot(h, jnp.concatenate([h, m], axis=0), NT)
            cross = y[:, B:] + dot(h, l, NT)
            inner.append(thirds(y[:, :B] + (dot(m, m, NT) + (cross + jnp.transpose(cross)))))
        turned = []
        for (ih, im, il), (h, m, l) in zip(inner, parts):
            main, rest = dot(beside(ih, im), jnp.concatenate([h, h], axis=0)), beside(ih, im)
            rest = dot(rest, jnp.concatenate([m, m], axis=0)) + dot(beside(ih, il), jnp.concatenate([l, h], axis=0))
            turned.append(main + rest)
        return tuple(1.5 * chain - 0.5 * y for chain, y in zip(chains, turned))

    chains = lax.fori_loop(0, ITERS, iterate, tuple(chains), unroll=ITERS)
    for half in range(2):
        rows = pl.ds(half * B, B)
        top, bottom = chains[half][:, :B], chains[half][:, B:]
        if share == 1:
            share_refs[0][rows, :] = jnp.where(flag_ref[2] == 0, chains[2 + half][:, :B], bottom)
        if share == 2:
            share_refs[0][rows, :], share_refs[1][rows, :] = chains[2 + half][:, :B], bottom
        if swap:
            first = flag_ref[0] == 1
            top, bottom = jnp.where(first, bottom, top), jnp.where(first, top, bottom)
        q_ref[0, rows, :] = beside(top, bottom)
        q_ref[1, rows, :] = chains[2 + half]
    if load:
        loading.wait()


def polar(flags, grams, swap=True, share=0, load=()):
    half = jax.ShapeDtypeStruct((2 * B, B), F32)
    return pl.pallas_call(
        functools.partial(polar_kernel, len(grams), swap, share, len(load)),
        in_specs=[SMEM] + [VMEM] * len(grams) + [ANY] * len(load),
        out_specs=[VMEM] * (1 + share + len(load)),
        out_shape=[jax.ShapeDtypeStruct((2, 2 * B, 2 * B), F32)]
        + [half] * share
        + [jax.ShapeDtypeStruct(x.shape, F32) for x in load],
        scratch_shapes=[pltpu.SemaphoreType.DMA] * len(load),
        compiler_params=pltpu.CompilerParams(vmem_limit_bytes=(40 if load else 20) * MIB),
        cost_estimate=SHORT,
        name="polar",
    )(flags, *grams, *load)


def turned(refs, q, rows):
    x = halves(beside(refs[0][rows, :], refs[1][rows, :]))
    return dot4(x, q) if len(q) == 3 else dot3(x, q)


def tiles(count, *cuts):
    bounds = [0, *cuts, count]
    return [pl.ds(i, min(TILE, hi - i)) for lo, hi in zip(bounds, bounds[1:]) for i in range(lo, hi, TILE)]


def rotate_kernel(early, t0_ref, b0_ref, t1_ref, b1_ref, q_ref, t1n_ref, left_ref, right_ref, b0n_ref, *parts):
    count = t0_ref.shape[0]
    q = [thirds(q_ref[pair]) for pair in range(2)]
    for rows in tiles(count, *([early] if parts else [])):
        top = turned((t0_ref, b0_ref), q[0], rows)
        bottom = turned((t1_ref, b1_ref), q[1], rows)
        t1n_ref[rows, :], left_ref[rows, :] = top[:, :B], top[:, B:]
        right_ref[rows, :], b0n_ref[rows, :] = bottom[:, :B], bottom[:, B:]
        if parts:
            late = int(rows.start >= early)
            part = pl.ds(rows.start - late * early, rows.size)
            parts[late][part, :], parts[2 + late][part, :] = top[:, :B], bottom[:, B:]


def rotate(blocks, q, early=0):
    count = blocks[0].shape[0]
    sizes = [count] * 4 + ([early, count - early] * 2 if early else [])
    return pl.pallas_call(
        functools.partial(rotate_kernel, early),
        in_specs=[VMEM] * 5,
        out_specs=[VMEM] * len(sizes),
        out_shape=[jax.ShapeDtypeStruct((size, B), F32) for size in sizes],
        compiler_params=pltpu.CompilerParams(vmem_limit_bytes=16 * MIB),
        cost_estimate=SHORT,
        name="rotate",
    )(*blocks, q)


def rotate_last_kernel(t0_ref, b0_ref, t1_ref, b1_ref, q_ref, out_ref, held_ref, sems):
    q = [halves(q_ref[pair]) for pair in range(2)]
    stores = []
    for i in range(sems.shape[0]):
        tile = out_ref.shape[0] // sems.shape[0]
        rows = pl.ds(i * tile, tile)
        held_ref[rows, : 2 * B] = turned((t0_ref, b0_ref), q[0], rows)
        held_ref[rows, 2 * B :] = turned((t1_ref, b1_ref), q[1], rows)
        stores.append(pltpu.make_async_copy(held_ref.at[rows], out_ref.at[rows], sems.at[i]))
        stores[-1].start()
    for store in stores:
        store.wait()


def rotate_last(blocks, q):
    count = blocks[0].shape[0]
    return pl.pallas_call(
        rotate_last_kernel,
        in_specs=[VMEM] * 5,
        out_specs=ANY,
        out_shape=jax.ShapeDtypeStruct((count, 4 * B), F32),
        scratch_shapes=[pltpu.VMEM((count, 4 * B), F32), pltpu.SemaphoreType.DMA((8,))],
        compiler_params=pltpu.CompilerParams(vmem_limit_bytes=16 * MIB),
        name="rotate_last",
    )(*blocks, q)


def rotate_part_kernel(columns, x_ref, q_ref, *outs):
    for pair in range(2):
        q = thirds(q_ref[pair, :, columns[pair] : columns[pair] + B])
        outs[pair][...] = dot4_narrow(halves(x_ref[:, 2 * B * pair : 2 * B * (pair + 1)]), q)


def rotate_part(x, q, columns):
    rows = x.shape[0]
    tile = min(TILE, rows)
    block = pl.BlockSpec((tile, B), lambda i: (i, 0))
    return pl.pallas_call(
        functools.partial(rotate_part_kernel, columns),
        grid=(rows // tile,),
        in_specs=[pl.BlockSpec((tile, 4 * B), lambda i: (i, 0)), pl.BlockSpec((2, 2 * B, 2 * B), lambda i: (0, 0, 0))],
        out_specs=[block] * 2,
        out_shape=[jax.ShapeDtypeStruct((rows, B), F32)] * 2,
        compiler_params=PARAMS,
        name="rotate_part",
    )(x, q)


def shifted(value, steps):
    count = lax.axis_size("pair")
    initial, last = (max(0, -steps), min(count, count - steps))
    return lax.ppermute(value, "pair", [(source, source + steps) for source in range(initial, last)])


def row_terms(g, relayed):
    rows, pairs = lax.axis_size("row"), lax.axis_size("pair")
    part = g + lax.ppermute(g, "row", [(r, r ^ 1) for r in range(rows)])
    if not relayed:
        return [part, lax.ppermute(part, "row", [(r, r ^ 2) for r in range(rows)])]
    both = ("pair", "row")
    relay = {0: RELAY, pairs - 1: pairs - 1 - RELAY}
    here = [p * rows + r for p in range(pairs) if p not in relay for r in range(rows)]
    ends = [(p * rows + r, via * rows + r) for p, via in relay.items() for r in range(rows)]
    hop = lax.ppermute(part, both, [(end, via ^ 2) for end, via in ends])
    direct = lax.ppermute(part, both, [(i, i ^ 2) for i in here])
    return [part, direct, lax.ppermute(hop, both, [(via, end) for end, via in ends])]


def sent(half):
    rows, pairs = lax.axis_size("row"), lax.axis_size("pair")
    right = [(p * rows + r, (p + 1) * rows + r) for p in range(pairs - 1) for r in range(0, rows, 2)]
    left = [(p * rows + r, (p - 1) * rows + r) for p in range(1, pairs) for r in range(1, rows, 2)]
    return lax.ppermute(half, ("pair", "row"), right + left)


def with_other(own, block):
    own, block = lax.optimization_barrier((own, block))
    return (own, lax.ppermute(own, "row", [(r, r ^ 1) for r in range(lax.axis_size("row"))])), block


def per_device(factor):
    position = lax.axis_index("pair")
    ends = [position == 0, position == lax.axis_size("pair") - 1, lax.axis_index("row") % 2 == 1]
    flags = jnp.stack(ends).astype(jnp.int32)
    ordered = jnp.array([1, 1, 0], jnp.int32)
    zero = jnp.zeros((2, GROWS, B), F32)

    count = factor.shape[0]
    early = count - LATE
    q, factor = polar(flags, row_terms(gram_first(factor), False), load=(factor,))
    left, right = rotate_part(factor, q, (B, 0))
    arrived = (shifted(right, 1), shifted(left, -1))
    t1, b0 = rotate_part(factor, q, (0, B))
    ahead = (shifted(t1, 1), shifted(b0, -1))

    g, t0, b1 = gram_next(flags, (left, right, b0, t1), arrived, (), zero)
    q, half_right, half_left = polar(flags, row_terms(g, True), share=2)
    rebuilt = (left, right, shifted(half_right, 1), shifted(half_left, -1))
    t1, left, right, b0, t1_early, t1_late, b0_early, b0_late = rotate([t0, b0, t1, b1], q, early)
    arrived, ahead = ahead, (shifted(t1_early, 1), shifted(b0_early, -1))

    g, t0, b1 = gram_next(flags * ordered, (left, right, b0, t1), arrived, rebuilt, zero)
    q, half = polar(flags, row_terms(g, True), share=1)
    half = sent(half)
    before = (left, right)
    (t1_late, b0_late), q = lax.optimization_barrier(((t1_late, b0_late), q))
    arrived = (shifted(t1_late, 1), shifted(b0_late, -1))
    t1, left, right, b0 = rotate([t0, b0, t1, b1], q)
    halves_q, left = with_other(half, left)
    rebuilt = (*before, *halves_q)

    g, t0, b1 = gram_next(flags, (left, right, b0, t1), ahead, rebuilt, zero)
    g, t0, b1 = gram_next(flags, (left, right, b0, t1), arrived, rebuilt, g, early, (t0, b1))
    (q,) = polar(flags, row_terms(g, False), swap=False)
    return rotate_last([t0, b0, t1, b1], q)


def solution(mesh):
    placed = (P("row", "pair"),)
    return jax.shard_map(
        per_device, mesh=mesh, in_specs=placed, out_specs=P("row", "pair"), check_vma=False
    )
```

```python
import functools
import jax
import jax.numpy as jnp
from jax import lax
from jax.experimental import pallas as pl
from jax.experimental.pallas import tpu as pltpu
from jax.sharding import PartitionSpec as P

B = 128
ITERS = 12
EPS = 1e-06
DAMPING = 0.04
TILE = 1024
GROWS = 136
LOADS = 4
LATE = 1024
RELAY = 5
F32 = jnp.float32
BF16 = jnp.bfloat16
LONG = pl.CostEstimate(flops=60 * 10**9, bytes_accessed=1 << 20, transcendentals=0)
SHORT = pl.CostEstimate(flops=5 * 10**9, bytes_accessed=1 << 20, transcendentals=0)
NONE = pl.CostEstimate(flops=10**6, bytes_accessed=1 << 10, transcendentals=0)
MIB = 1024 * 1024
PARAMS = pltpu.CompilerParams(vmem_limit_bytes=20 * MIB)
NN = (((1,), (0,)), ((), ()))
NT = (((1,), (1,)), ((), ()))
TN = (((0,), (0,)), ((), ()))
VMEM = pl.BlockSpec(memory_space=pltpu.VMEM)
ANY = pl.BlockSpec(memory_space=pl.ANY)
SMEM = pl.BlockSpec(memory_space=pltpu.SMEM)


def halves(value):
    high = value.astype(BF16)
    return high, (value - high.astype(F32)).astype(BF16)


def dot(a, b, dims=NN):
    return lax.dot_general(a, b, dims, preferred_element_type=F32)


def dot3(a, b, dims=NN):
    return dot(a[0], b[0], dims) + (dot(a[0], b[1], dims) + dot(a[1], b[0], dims))


def beside(a, b):
    return jnp.concatenate([a, b], axis=1)


def thirds(value):
    high = value.astype(BF16)
    rest = value - high.astype(F32)
    middle = rest.astype(BF16)
    return high, middle, (rest - middle.astype(F32)).astype(BF16)


def dot4(a, b):
    return dot(a[0], b[0]) + ((dot(a[0], b[1]) + dot(a[1], b[0])) + dot(a[0], b[2]))


def dot3_narrow(a, b):
    y = dot(a[0], beside(*b))
    return y[:, :B] + (y[:, B:] + dot(a[1], b[0]))


def dot4_narrow(a, b):
    y = dot(a[0], beside(b[0], b[1]))
    return y[:, :B] + (y[:, B:] + (dot(a[1], b[0]) + dot(a[0], b[2])))


def add_gram(g_ref, pair, top, bottom):
    product = dot(beside(*halves(top)), beside(*halves(bottom)), TN)
    g_ref[pair, :B, :] += (product[:B, :B] + product[B:, B:]) + (product[:B, B:] + product[B:, :B])
    g_ref[pair, B : B + 1, :] += jnp.sum(top * top, axis=0, keepdims=True)
    g_ref[pair, B + 1 : B + 2, :] += jnp.sum(bottom * bottom, axis=0, keepdims=True)


def gram_first_kernel(x_ref, g_ref, copy_ref, sems):
    tile = x_ref.shape[0] // LOADS
    loads = []
    for i in range(LOADS):
        rows = pl.ds(i * tile, tile)
        loads.append(pltpu.make_async_copy(x_ref.at[rows], copy_ref.at[rows], sems.at[i]))
        loads[-1].start()
    g_ref[...] = jnp.zeros_like(g_ref)
    for i in range(LOADS):
        loads[i].wait()
        for pair in range(2):
            base = 2 * B * pair
            rows = slice(i * tile, (i + 1) * tile)
            add_gram(g_ref, pair, copy_ref[rows, base : base + B], copy_ref[rows, base + B : base + 2 * B])


def gram_first(x):
    return pl.pallas_call(
        gram_first_kernel,
        in_specs=[ANY],
        out_specs=VMEM,
        out_shape=jax.ShapeDtypeStruct((2, GROWS, B), F32),
        scratch_shapes=[pltpu.VMEM(x.shape, F32), pltpu.SemaphoreType.DMA((LOADS,))],
        compiler_params=pltpu.CompilerParams(vmem_limit_bytes=52 * MIB),
        name="gram_first",
    )(x)


def gram_next_kernel(rebuild, fine, flag_ref, first_ref, last_ref, b0_ref, t1_ref, in_top_ref, in_bottom_ref, *rest):
    if rebuild:
        prev_left_ref, prev_right_ref, own_ref, other_ref, *rest = rest
    g_in_ref, *_, g_ref, t0_ref, b1_ref = rest

    @pl.when(pl.program_id(0) == 0)
    def _():
        g_ref[...] = g_in_ref[...]

    in_top, in_bottom = in_top_ref[...], in_bottom_ref[...]
    if rebuild:
        q_top = jnp.where(flag_ref[2] == 0, own_ref[...], other_ref[...])
        q_bottom = jnp.where(flag_ref[2] == 0, other_ref[...], own_ref[...])
        product, parts = (dot4_narrow, thirds) if fine else (dot3_narrow, halves)
        in_top = product(halves(beside(in_top, prev_left_ref[...])), parts(q_top))
        in_bottom = product(halves(beside(prev_right_ref[...], in_bottom)), parts(q_bottom))
    t0 = jnp.where(flag_ref[0] == 1, first_ref[...], in_top)
    b1 = jnp.where(flag_ref[1] == 1, last_ref[...], in_bottom)
    t0_ref[...] = t0
    b1_ref[...] = b1
    add_gram(g_ref, 0, t0, b0_ref[...])
    add_gram(g_ref, 1, t1_ref[...], b1)


def gram_next(flags, blocks, arrived, rebuilt, g_in, start=0, written=(), fine=True):
    rows, count = blocks[0].shape[0], arrived[0].shape[0]
    tile = max(t for t in (128, 256, 512, 896, 1024) if count % t == 0 and start % t == 0)
    offset = start // tile
    block = pl.BlockSpec((tile, B), lambda i: (i + offset, 0))
    part = pl.BlockSpec((tile, B), lambda i: (i, 0))
    half = pl.BlockSpec((2 * B, B), lambda i: (0, 0))
    gram = pl.BlockSpec((2, GROWS, B), lambda i: (0, 0, 0))
    extra = [block, block, half, half] if rebuilt else []
    in_specs = [SMEM] + [block] * 4 + [part] * 2 + extra + [gram] + [ANY] * len(written)
    return pl.pallas_call(
        functools.partial(gram_next_kernel, bool(rebuilt), fine),
        grid=(count // tile,),
        in_specs=in_specs,
        out_specs=[gram, block, block],
        out_shape=[jax.ShapeDtypeStruct((2, GROWS, B), F32)] + [jax.ShapeDtypeStruct((rows, B), F32)] * 2,
        input_output_aliases={len(in_specs) - 2 + i: 1 + i for i in range(len(written))},
        compiler_params=PARAMS,
        cost_estimate=LONG if count == rows else NONE,
        name="gram_next",
    )(flags, *blocks, *arrived, *rebuilt, g_in, *written)


def polar_kernel(terms, swap, share, load, flag_ref, *refs):
    g_refs, refs = refs[:terms], refs[terms:]
    if load:
        x_ref, q_ref, copy_ref, sem = refs
        loading = pltpu.make_async_copy(x_ref, copy_ref, sem)
        loading.start()
    else:
        q_ref, *share_refs = refs
    total = g_refs[0][...]
    for g_ref in g_refs[1:]:
        total = total + g_ref[...]
    eye = (lax.broadcasted_iota(jnp.int32, (B, B), 0) == lax.broadcasted_iota(jnp.int32, (B, B), 1)).astype(F32)
    chains = []
    for pair in range(2):
        gram = total[pair, :B]
        norm_top = jnp.transpose(jnp.broadcast_to(total[pair, B : B + 1], (B, B)))
        norm_bottom = jnp.broadcast_to(total[pair, B + 1 : B + 2], (B, B))
        differ = norm_top - norm_bottom
        both = norm_top + norm_bottom + EPS
        radius = jnp.sqrt(differ * differ + 4.0 * gram * gram)
        denominator = differ * differ + jnp.abs(differ) * radius + DAMPING * both * both
        coupling = -2.0 * gram * differ / denominator
        scale = lax.rsqrt(1.0 + jnp.sum(coupling * coupling, keepdims=True))
        chains.append(beside(eye, coupling) * scale)
        chains.append(beside(-jnp.transpose(coupling), eye) * scale)

    def iterate(_, chains):
        parts = [thirds(chain) for chain in chains]
        inner = []
        for h, m, l in parts:
            y = dot(h, jnp.concatenate([h, m], axis=0), NT)
            cross = y[:, B:] + dot(h, l, NT)
            inner.append(thirds(y[:, :B] + (dot(m, m, NT) + (cross + jnp.transpose(cross)))))
        turned = []
        for (ih, im, il), (h, m, l) in zip(inner, parts):
            main, rest = dot(beside(ih, im), jnp.concatenate([h, h], axis=0)), beside(ih, im)
            rest = dot(rest, jnp.concatenate([m, m], axis=0)) + dot(beside(ih, il), jnp.concatenate([l, h], axis=0))
            turned.append(main + rest)
        return tuple(1.5 * chain - 0.5 * y for chain, y in zip(chains, turned))

    chains = lax.fori_loop(0, ITERS, iterate, tuple(chains), unroll=ITERS)
    for half in range(2):
        rows = pl.ds(half * B, B)
        top, bottom = chains[half][:, :B], chains[half][:, B:]
        if share == 1:
            share_refs[0][rows, :] = jnp.where(flag_ref[2] == 0, chains[2 + half][:, :B], bottom)
        if share == 2:
            share_refs[0][rows, :], share_refs[1][rows, :] = chains[2 + half][:, :B], bottom
        if swap:
            first = flag_ref[0] == 1
            top, bottom = jnp.where(first, bottom, top), jnp.where(first, top, bottom)
        q_ref[0, rows, :] = beside(top, bottom)
        q_ref[1, rows, :] = chains[2 + half]
    if load:
        loading.wait()


def polar(flags, grams, swap=True, share=0, load=()):
    half = jax.ShapeDtypeStruct((2 * B, B), F32)
    return pl.pallas_call(
        functools.partial(polar_kernel, len(grams), swap, share, len(load)),
        in_specs=[SMEM] + [VMEM] * len(grams) + [ANY] * len(load),
        out_specs=[VMEM] * (1 + share + len(load)),
        out_shape=[jax.ShapeDtypeStruct((2, 2 * B, 2 * B), F32)]
        + [half] * share
        + [jax.ShapeDtypeStruct(x.shape, F32) for x in load],
        scratch_shapes=[pltpu.SemaphoreType.DMA] * len(load),
        compiler_params=pltpu.CompilerParams(vmem_limit_bytes=(40 if load else 20) * MIB),
        cost_estimate=SHORT,
        name="polar",
    )(flags, *grams, *load)


def turned(refs, q, rows):
    x = halves(beside(refs[0][rows, :], refs[1][rows, :]))
    return dot4(x, q) if len(q) == 3 else dot3(x, q)


def tiles(count, *cuts):
    bounds = [0, *cuts, count]
    return [pl.ds(i, min(TILE, hi - i)) for lo, hi in zip(bounds, bounds[1:]) for i in range(lo, hi, TILE)]


def rotate_kernel(early, fine, t0_ref, b0_ref, t1_ref, b1_ref, q_ref, t1n_ref, left_ref, right_ref, b0n_ref, *parts):
    count = t0_ref.shape[0]
    q = [(thirds if fine else halves)(q_ref[pair]) for pair in range(2)]
    for rows in tiles(count, *([early] if parts else [])):
        top = turned((t0_ref, b0_ref), q[0], rows)
        bottom = turned((t1_ref, b1_ref), q[1], rows)
        t1n_ref[rows, :], left_ref[rows, :] = top[:, :B], top[:, B:]
        right_ref[rows, :], b0n_ref[rows, :] = bottom[:, :B], bottom[:, B:]
        if parts:
            late = int(rows.start >= early)
            part = pl.ds(rows.start - late * early, rows.size)
            parts[late][part, :], parts[2 + late][part, :] = top[:, :B], bottom[:, B:]


def rotate(blocks, q, early=0, fine=True):
    count = blocks[0].shape[0]
    sizes = [count] * 4 + ([early, count - early] * 2 if early else [])
    return pl.pallas_call(
        functools.partial(rotate_kernel, early, fine),
        in_specs=[VMEM] * 5,
        out_specs=[VMEM] * len(sizes),
        out_shape=[jax.ShapeDtypeStruct((size, B), F32) for size in sizes],
        compiler_params=pltpu.CompilerParams(vmem_limit_bytes=16 * MIB),
        cost_estimate=SHORT,
        name="rotate",
    )(*blocks, q)


def rotate_last_kernel(t0_ref, b0_ref, t1_ref, b1_ref, q_ref, out_ref, held_ref, sems):
    q = [halves(q_ref[pair]) for pair in range(2)]
    stores = []
    for i in range(sems.shape[0]):
        tile = out_ref.shape[0] // sems.shape[0]
        rows = pl.ds(i * tile, tile)
        held_ref[rows, : 2 * B] = turned((t0_ref, b0_ref), q[0], rows)
        held_ref[rows, 2 * B :] = turned((t1_ref, b1_ref), q[1], rows)
        stores.append(pltpu.make_async_copy(held_ref.at[rows], out_ref.at[rows], sems.at[i]))
        stores[-1].start()
    for store in stores:
        store.wait()


def rotate_last(blocks, q):
    count = blocks[0].shape[0]
    return pl.pallas_call(
        rotate_last_kernel,
        in_specs=[VMEM] * 5,
        out_specs=ANY,
        out_shape=jax.ShapeDtypeStruct((count, 4 * B), F32),
        scratch_shapes=[pltpu.VMEM((count, 4 * B), F32), pltpu.SemaphoreType.DMA((8,))],
        compiler_params=pltpu.CompilerParams(vmem_limit_bytes=16 * MIB),
        name="rotate_last",
    )(*blocks, q)


def rotate_part_kernel(columns, x_ref, q_ref, *outs):
    for pair in range(2):
        q = thirds(q_ref[pair, :, columns[pair] : columns[pair] + B])
        outs[pair][...] = dot4_narrow(halves(x_ref[:, 2 * B * pair : 2 * B * (pair + 1)]), q)


def rotate_part(x, q, columns):
    rows = x.shape[0]
    tile = min(TILE, rows)
    block = pl.BlockSpec((tile, B), lambda i: (i, 0))
    return pl.pallas_call(
        functools.partial(rotate_part_kernel, columns),
        grid=(rows // tile,),
        in_specs=[pl.BlockSpec((tile, 4 * B), lambda i: (i, 0)), pl.BlockSpec((2, 2 * B, 2 * B), lambda i: (0, 0, 0))],
        out_specs=[block] * 2,
        out_shape=[jax.ShapeDtypeStruct((rows, B), F32)] * 2,
        compiler_params=PARAMS,
        name="rotate_part",
    )(x, q)


def shifted(value, steps):
    count = lax.axis_size("pair")
    initial, last = (max(0, -steps), min(count, count - steps))
    return lax.ppermute(value, "pair", [(source, source + steps) for source in range(initial, last)])


def row_terms(g, relayed):
    rows, pairs = lax.axis_size("row"), lax.axis_size("pair")
    part = g + lax.ppermute(g, "row", [(r, r ^ 1) for r in range(rows)])
    if not relayed:
        return [part, lax.ppermute(part, "row", [(r, r ^ 2) for r in range(rows)])]
    both = ("pair", "row")
    relay = {0: RELAY, pairs - 1: pairs - 1 - RELAY}
    here = [p * rows + r for p in range(pairs) if p not in relay for r in range(rows)]
    ends = [(p * rows + r, via * rows + r) for p, via in relay.items() for r in range(rows)]
    hop = lax.ppermute(part, both, [(end, via ^ 2) for end, via in ends])
    direct = lax.ppermute(part, both, [(i, i ^ 2) for i in here])
    return [part, direct, lax.ppermute(hop, both, [(via, end) for end, via in ends])]


def sent(half):
    rows, pairs = lax.axis_size("row"), lax.axis_size("pair")
    right = [(p * rows + r, (p + 1) * rows + r) for p in range(pairs - 1) for r in range(0, rows, 2)]
    left = [(p * rows + r, (p - 1) * rows + r) for p in range(1, pairs) for r in range(1, rows, 2)]
    return lax.ppermute(half, ("pair", "row"), right + left)


def with_other(own, block):
    own, block = lax.optimization_barrier((own, block))
    return (own, lax.ppermute(own, "row", [(r, r ^ 1) for r in range(lax.axis_size("row"))])), block


def per_device(factor):
    position = lax.axis_index("pair")
    ends = [position == 0, position == lax.axis_size("pair") - 1, lax.axis_index("row") % 2 == 1]
    flags = jnp.stack(ends).astype(jnp.int32)
    ordered = jnp.array([1, 1, 0], jnp.int32)
    zero = jnp.zeros((2, GROWS, B), F32)

    count = factor.shape[0]
    early = count - LATE
    q, factor = polar(flags, row_terms(gram_first(factor), False), load=(factor,))
    left, right = rotate_part(factor, q, (B, 0))
    arrived = (shifted(right, 1), shifted(left, -1))
    t1, b0 = rotate_part(factor, q, (0, B))
    ahead = (shifted(t1, 1), shifted(b0, -1))

    g, t0, b1 = gram_next(flags, (left, right, b0, t1), arrived, (), zero)
    q, half_right, half_left = polar(flags, row_terms(g, True), share=2)
    rebuilt = (left, right, shifted(half_right, 1), shifted(half_left, -1))
    t1, left, right, b0, t1_early, t1_late, b0_early, b0_late = rotate([t0, b0, t1, b1], q, early)
    arrived, ahead = ahead, (shifted(t1_early, 1), shifted(b0_early, -1))

    g, t0, b1 = gram_next(flags * ordered, (left, right, b0, t1), arrived, rebuilt, zero)
    q, half = polar(flags, row_terms(g, True), share=1)
    half = sent(half)
    before = (left, right)
    (t1_late, b0_late), q = lax.optimization_barrier(((t1_late, b0_late), q))
    arrived = (shifted(t1_late, 1), shifted(b0_late, -1))
    t1, left, right, b0 = rotate([t0, b0, t1, b1], q, fine=False)
    halves_q, left = with_other(half, left)
    rebuilt = (*before, *halves_q)

    g, t0, b1 = gram_next(flags, (left, right, b0, t1), ahead, rebuilt, zero, fine=False)
    g, t0, b1 = gram_next(flags, (left, right, b0, t1), arrived, rebuilt, g, early, (t0, b1), fine=False)
    (q,) = polar(flags, row_terms(g, False), swap=False)
    return rotate_last([t0, b0, t1, b1], q)


def solution(mesh):
    placed = (P("row", "pair"),)
    return jax.shard_map(
        per_device, mesh=mesh, in_specs=placed, out_specs=P("row", "pair"), check_vma=False
    )
```

```python
import functools
import jax
import jax.numpy as jnp
from jax import lax
from jax.experimental import pallas as pl
from jax.experimental.pallas import tpu as pltpu
from jax.sharding import PartitionSpec as P

B = 128
ITERS = 12
EPS = 1e-06
DAMPING = 0.04
TILE = 1024
GROWS = 136
LOADS = 4
LATE = 1024
RELAY = 5
F32 = jnp.float32
BF16 = jnp.bfloat16
LONG = pl.CostEstimate(flops=60 * 10**9, bytes_accessed=1 << 20, transcendentals=0)
SHORT = pl.CostEstimate(flops=5 * 10**9, bytes_accessed=1 << 20, transcendentals=0)
NONE = pl.CostEstimate(flops=10**6, bytes_accessed=1 << 10, transcendentals=0)
MIB = 1024 * 1024
PARAMS = pltpu.CompilerParams(vmem_limit_bytes=20 * MIB)
NN = (((1,), (0,)), ((), ()))
NT = (((1,), (1,)), ((), ()))
TN = (((0,), (0,)), ((), ()))
VMEM = pl.BlockSpec(memory_space=pltpu.VMEM)
ANY = pl.BlockSpec(memory_space=pl.ANY)
SMEM = pl.BlockSpec(memory_space=pltpu.SMEM)


def halves(value):
    high = value.astype(BF16)
    return high, (value - high.astype(F32)).astype(BF16)


def dot(a, b, dims=NN):
    return lax.dot_general(a, b, dims, preferred_element_type=F32)


def dot3(a, b, dims=NN):
    return dot(a[0], b[0], dims) + (dot(a[0], b[1], dims) + dot(a[1], b[0], dims))


def beside(a, b):
    return jnp.concatenate([a, b], axis=1)


def thirds(value):
    high = value.astype(BF16)
    rest = value - high.astype(F32)
    middle = rest.astype(BF16)
    return high, middle, (rest - middle.astype(F32)).astype(BF16)


def dot4(a, b):
    return dot(a[0], b[0]) + ((dot(a[0], b[1]) + dot(a[1], b[0])) + dot(a[0], b[2]))


def dot3_narrow(a, b):
    y = dot(a[0], beside(*b))
    return y[:, :B] + (y[:, B:] + dot(a[1], b[0]))


def dot4_narrow(a, b):
    y = dot(a[0], beside(b[0], b[1]))
    return y[:, :B] + (y[:, B:] + (dot(a[1], b[0]) + dot(a[0], b[2])))


def add_gram(g_ref, pair, top, bottom):
    product = dot(beside(*halves(top)), beside(*halves(bottom)), TN)
    g_ref[pair, :B, :] += (product[:B, :B] + product[B:, B:]) + (product[:B, B:] + product[B:, :B])
    g_ref[pair, B : B + 1, :] += jnp.sum(top * top, axis=0, keepdims=True)
    g_ref[pair, B + 1 : B + 2, :] += jnp.sum(bottom * bottom, axis=0, keepdims=True)


def gram_first_kernel(x_ref, g_ref, copy_ref, sems):
    tile = x_ref.shape[0] // LOADS
    loads = []
    for i in range(LOADS):
        rows = pl.ds(i * tile, tile)
        loads.append(pltpu.make_async_copy(x_ref.at[rows], copy_ref.at[rows], sems.at[i]))
        loads[-1].start()
    g_ref[...] = jnp.zeros_like(g_ref)
    for i in range(LOADS):
        loads[i].wait()
        for pair in range(2):
            base = 2 * B * pair
            rows = slice(i * tile, (i + 1) * tile)
            add_gram(g_ref, pair, copy_ref[rows, base : base + B], copy_ref[rows, base + B : base + 2 * B])


def gram_first(x):
    return pl.pallas_call(
        gram_first_kernel,
        in_specs=[ANY],
        out_specs=VMEM,
        out_shape=jax.ShapeDtypeStruct((2, GROWS, B), F32),
        scratch_shapes=[pltpu.VMEM(x.shape, F32), pltpu.SemaphoreType.DMA((LOADS,))],
        compiler_params=pltpu.CompilerParams(vmem_limit_bytes=52 * MIB),
        name="gram_first",
    )(x)


def gram_next_kernel(rebuild, fine, flag_ref, first_ref, last_ref, b0_ref, t1_ref, in_top_ref, in_bottom_ref, *rest):
    if rebuild:
        prev_left_ref, prev_right_ref, own_ref, other_ref, *rest = rest
    g_in_ref, *_, g_ref, t0_ref, b1_ref = rest

    @pl.when(pl.program_id(0) == 0)
    def _():
        g_ref[...] = g_in_ref[...]

    in_top, in_bottom = in_top_ref[...], in_bottom_ref[...]
    if rebuild:
        q_top = jnp.where(flag_ref[2] == 0, own_ref[...], other_ref[...])
        q_bottom = jnp.where(flag_ref[2] == 0, other_ref[...], own_ref[...])
        product, parts = (dot4_narrow, thirds) if fine else (dot3_narrow, halves)
        in_top = product(halves(beside(in_top, prev_left_ref[...])), parts(q_top))
        in_bottom = product(halves(beside(prev_right_ref[...], in_bottom)), parts(q_bottom))
    t0 = jnp.where(flag_ref[0] == 1, first_ref[...], in_top)
    b1 = jnp.where(flag_ref[1] == 1, last_ref[...], in_bottom)
    t0_ref[...] = t0
    b1_ref[...] = b1
    add_gram(g_ref, 0, t0, b0_ref[...])
    add_gram(g_ref, 1, t1_ref[...], b1)


def gram_next(flags, blocks, arrived, rebuilt, g_in, start=0, written=(), fine=True):
    rows, count = blocks[0].shape[0], arrived[0].shape[0]
    tile = max(t for t in (128, 256, 512, 896, 1024) if count % t == 0 and start % t == 0)
    offset = start // tile
    block = pl.BlockSpec((tile, B), lambda i: (i + offset, 0))
    part = pl.BlockSpec((tile, B), lambda i: (i, 0))
    half = pl.BlockSpec((2 * B, B), lambda i: (0, 0))
    gram = pl.BlockSpec((2, GROWS, B), lambda i: (0, 0, 0))
    extra = [block, block, half, half] if rebuilt else []
    in_specs = [SMEM] + [block] * 4 + [part] * 2 + extra + [gram] + [ANY] * len(written)
    return pl.pallas_call(
        functools.partial(gram_next_kernel, bool(rebuilt), fine),
        grid=(count // tile,),
        in_specs=in_specs,
        out_specs=[gram, block, block],
        out_shape=[jax.ShapeDtypeStruct((2, GROWS, B), F32)] + [jax.ShapeDtypeStruct((rows, B), F32)] * 2,
        input_output_aliases={len(in_specs) - 2 + i: 1 + i for i in range(len(written))},
        compiler_params=PARAMS,
        cost_estimate=LONG if count == rows else NONE,
        name="gram_next",
    )(flags, *blocks, *arrived, *rebuilt, g_in, *written)


def polar_kernel(terms, swap, share, load, flag_ref, *refs):
    g_refs, refs = refs[:terms], refs[terms:]
    if load:
        x_ref, q_ref, copy_ref, sem = refs
        loading = pltpu.make_async_copy(x_ref, copy_ref, sem)
        loading.start()
    else:
        q_ref, *share_refs = refs
    total = g_refs[0][...]
    for g_ref in g_refs[1:]:
        total = total + g_ref[...]
    eye = (lax.broadcasted_iota(jnp.int32, (B, B), 0) == lax.broadcasted_iota(jnp.int32, (B, B), 1)).astype(F32)
    chains = []
    for pair in range(2):
        gram = total[pair, :B]
        norm_top = jnp.transpose(jnp.broadcast_to(total[pair, B : B + 1], (B, B)))
        norm_bottom = jnp.broadcast_to(total[pair, B + 1 : B + 2], (B, B))
        differ = norm_top - norm_bottom
        both = norm_top + norm_bottom + EPS
        radius = jnp.sqrt(differ * differ + 4.0 * gram * gram)
        denominator = differ * differ + jnp.abs(differ) * radius + DAMPING * both * both
        coupling = -2.0 * gram * differ / denominator
        scale = lax.rsqrt(1.0 + jnp.sum(coupling * coupling, keepdims=True))
        chains.append(beside(eye, coupling) * scale)
        chains.append(beside(-jnp.transpose(coupling), eye) * scale)

    def iterate(_, chains):
        parts = [thirds(chain) for chain in chains]
        inner = []
        for h, m, l in parts:
            y = dot(h, jnp.concatenate([h, m], axis=0), NT)
            cross = y[:, B:] + dot(h, l, NT)
            inner.append(thirds(y[:, :B] + (dot(m, m, NT) + (cross + jnp.transpose(cross)))))
        turned = []
        for (ih, im, il), (h, m, l) in zip(inner, parts):
            main, rest = dot(beside(ih, im), jnp.concatenate([h, h], axis=0)), beside(ih, im)
            rest = dot(rest, jnp.concatenate([m, m], axis=0)) + dot(beside(ih, il), jnp.concatenate([l, h], axis=0))
            turned.append(main + rest)
        return tuple(1.5 * chain - 0.5 * y for chain, y in zip(chains, turned))

    chains = lax.fori_loop(0, ITERS, iterate, tuple(chains), unroll=ITERS)
    for half in range(2):
        rows = pl.ds(half * B, B)
        top, bottom = chains[half][:, :B], chains[half][:, B:]
        if share == 1:
            share_refs[0][rows, :] = jnp.where(flag_ref[2] == 0, chains[2 + half][:, :B], bottom)
        if share == 2:
            share_refs[0][rows, :], share_refs[1][rows, :] = chains[2 + half][:, :B], bottom
        if swap:
            first = flag_ref[0] == 1
            top, bottom = jnp.where(first, bottom, top), jnp.where(first, top, bottom)
        q_ref[0, rows, :] = beside(top, bottom)
        q_ref[1, rows, :] = chains[2 + half]
    if load:
        loading.wait()


def polar(flags, grams, swap=True, share=0, load=()):
    half = jax.ShapeDtypeStruct((2 * B, B), F32)
    return pl.pallas_call(
        functools.partial(polar_kernel, len(grams), swap, share, len(load)),
        in_specs=[SMEM] + [VMEM] * len(grams) + [ANY] * len(load),
        out_specs=[VMEM] * (1 + share + len(load)),
        out_shape=[jax.ShapeDtypeStruct((2, 2 * B, 2 * B), F32)]
        + [half] * share
        + [jax.ShapeDtypeStruct(x.shape, F32) for x in load],
        scratch_shapes=[pltpu.SemaphoreType.DMA] * len(load),
        compiler_params=pltpu.CompilerParams(vmem_limit_bytes=(40 if load else 20) * MIB),
        cost_estimate=SHORT,
        name="polar",
    )(flags, *grams, *load)


def turned(refs, q, rows):
    x = halves(beside(refs[0][rows, :], refs[1][rows, :]))
    return dot4(x, q) if len(q) == 3 else dot3(x, q)


def tiles(count, *cuts):
    bounds = [0, *cuts, count]
    return [pl.ds(i, min(TILE, hi - i)) for lo, hi in zip(bounds, bounds[1:]) for i in range(lo, hi, TILE)]


def rotate_kernel(early, fine, t0_ref, b0_ref, t1_ref, b1_ref, q_ref, t1n_ref, left_ref, right_ref, b0n_ref, *parts):
    count = t0_ref.shape[0]
    q = [(thirds if fine else halves)(q_ref[pair]) for pair in range(2)]
    for rows in tiles(count, *([early] if parts else [])):
        top = turned((t0_ref, b0_ref), q[0], rows)
        bottom = turned((t1_ref, b1_ref), q[1], rows)
        t1n_ref[rows, :], left_ref[rows, :] = top[:, :B], top[:, B:]
        right_ref[rows, :], b0n_ref[rows, :] = bottom[:, :B], bottom[:, B:]
        if parts:
            late = int(rows.start >= early)
            part = pl.ds(rows.start - late * early, rows.size)
            parts[late][part, :], parts[2 + late][part, :] = top[:, :B], bottom[:, B:]


def rotate(blocks, q, early=0, fine=True):
    count = blocks[0].shape[0]
    sizes = [count] * 4 + ([early, count - early] * 2 if early else [])
    return pl.pallas_call(
        functools.partial(rotate_kernel, early, fine),
        in_specs=[VMEM] * 5,
        out_specs=[VMEM] * len(sizes),
        out_shape=[jax.ShapeDtypeStruct((size, B), F32) for size in sizes],
        compiler_params=pltpu.CompilerParams(vmem_limit_bytes=16 * MIB),
        cost_estimate=SHORT,
        name="rotate",
    )(*blocks, q)


def rotate_last_kernel(t0_ref, b0_ref, t1_ref, b1_ref, q_ref, out_ref):
    rows = pl.ds(0, out_ref.shape[0])
    out_ref[:, : 2 * B] = turned((t0_ref, b0_ref), halves(q_ref[0]), rows)
    out_ref[:, 2 * B :] = turned((t1_ref, b1_ref), halves(q_ref[1]), rows)


def rotate_last(blocks, q):
    count = blocks[0].shape[0]
    tile = min(TILE, count)
    return pl.pallas_call(
        rotate_last_kernel,
        grid=(count // tile,),
        in_specs=[pl.BlockSpec((tile, B), lambda i: (i, 0))] * 4 + [VMEM],
        out_specs=pl.BlockSpec((tile, 4 * B), lambda i: (i, 0)),
        out_shape=jax.ShapeDtypeStruct((count, 4 * B), F32),
        compiler_params=PARAMS,
        name="rotate_last",
    )(*blocks, q)


def rotate_part_kernel(columns, x_ref, q_ref, *outs):
    for pair in range(2):
        q = thirds(q_ref[pair, :, columns[pair] : columns[pair] + B])
        outs[pair][...] = dot4_narrow(halves(x_ref[:, 2 * B * pair : 2 * B * (pair + 1)]), q)


def rotate_part(x, q, columns):
    rows = x.shape[0]
    tile = min(TILE, rows)
    block = pl.BlockSpec((tile, B), lambda i: (i, 0))
    return pl.pallas_call(
        functools.partial(rotate_part_kernel, columns),
        grid=(rows // tile,),
        in_specs=[pl.BlockSpec((tile, 4 * B), lambda i: (i, 0)), pl.BlockSpec((2, 2 * B, 2 * B), lambda i: (0, 0, 0))],
        out_specs=[block] * 2,
        out_shape=[jax.ShapeDtypeStruct((rows, B), F32)] * 2,
        compiler_params=PARAMS,
        name="rotate_part",
    )(x, q)


def shifted(value, steps):
    count = lax.axis_size("pair")
    initial, last = (max(0, -steps), min(count, count - steps))
    return lax.ppermute(value, "pair", [(source, source + steps) for source in range(initial, last)])


def row_terms(g, relayed):
    rows, pairs = lax.axis_size("row"), lax.axis_size("pair")
    part = g + lax.ppermute(g, "row", [(r, r ^ 1) for r in range(rows)])
    if not relayed:
        return [part, lax.ppermute(part, "row", [(r, r ^ 2) for r in range(rows)])]
    both = ("pair", "row")
    relay = {0: RELAY, pairs - 1: pairs - 1 - RELAY}
    here = [p * rows + r for p in range(pairs) if p not in relay for r in range(rows)]
    ends = [(p * rows + r, via * rows + r) for p, via in relay.items() for r in range(rows)]
    hop = lax.ppermute(part, both, [(end, via ^ 2) for end, via in ends])
    direct = lax.ppermute(part, both, [(i, i ^ 2) for i in here])
    return [part, direct, lax.ppermute(hop, both, [(via, end) for end, via in ends])]


def sent(half):
    rows, pairs = lax.axis_size("row"), lax.axis_size("pair")
    right = [(p * rows + r, (p + 1) * rows + r) for p in range(pairs - 1) for r in range(0, rows, 2)]
    left = [(p * rows + r, (p - 1) * rows + r) for p in range(1, pairs) for r in range(1, rows, 2)]
    return lax.ppermute(half, ("pair", "row"), right + left)


def with_other(own, block):
    own, block = lax.optimization_barrier((own, block))
    return (own, lax.ppermute(own, "row", [(r, r ^ 1) for r in range(lax.axis_size("row"))])), block


def per_device(factor):
    position = lax.axis_index("pair")
    ends = [position == 0, position == lax.axis_size("pair") - 1, lax.axis_index("row") % 2 == 1]
    flags = jnp.stack(ends).astype(jnp.int32)
    ordered = jnp.array([1, 1, 0], jnp.int32)
    zero = jnp.zeros((2, GROWS, B), F32)

    count = factor.shape[0]
    early = count - LATE
    q, factor = polar(flags, row_terms(gram_first(factor), False), load=(factor,))
    left, right = rotate_part(factor, q, (B, 0))
    arrived = (shifted(right, 1), shifted(left, -1))
    t1, b0 = rotate_part(factor, q, (0, B))
    ahead = (shifted(t1, 1), shifted(b0, -1))

    g, t0, b1 = gram_next(flags, (left, right, b0, t1), arrived, (), zero)
    q, half_right, half_left = polar(flags, row_terms(g, True), share=2)
    rebuilt = (left, right, shifted(half_right, 1), shifted(half_left, -1))
    t1, left, right, b0, t1_early, t1_late, b0_early, b0_late = rotate([t0, b0, t1, b1], q, early)
    arrived, ahead = ahead, (shifted(t1_early, 1), shifted(b0_early, -1))

    g, t0, b1 = gram_next(flags * ordered, (left, right, b0, t1), arrived, rebuilt, zero)
    q, half = polar(flags, row_terms(g, True), share=1)
    half = sent(half)
    before = (left, right)
    (t1_late, b0_late), q = lax.optimization_barrier(((t1_late, b0_late), q))
    arrived = (shifted(t1_late, 1), shifted(b0_late, -1))
    t1, left, right, b0 = rotate([t0, b0, t1, b1], q, fine=False)
    halves_q, left = with_other(half, left)
    rebuilt = (*before, *halves_q)

    g, t0, b1 = gram_next(flags, (left, right, b0, t1), ahead, rebuilt, zero, fine=False)
    g, t0, b1 = gram_next(flags, (left, right, b0, t1), arrived, rebuilt, g, early, (t0, b1), fine=False)
    (q,) = polar(flags, row_terms(g, False), swap=False)
    return rotate_last([t0, b0, t1, b1], q)


def solution(mesh):
    placed = (P("row", "pair"),)
    return jax.shard_map(
        per_device, mesh=mesh, in_specs=placed, out_specs=P("row", "pair"), check_vma=False
    )
```

```python
import functools
import jax
import jax.numpy as jnp
from jax import lax
from jax.experimental import pallas as pl
from jax.experimental.pallas import tpu as pltpu
from jax.sharding import PartitionSpec as P

B = 128
ITERS = 12
EPS = 1e-06
DAMPING = 0.04
TILE = 1024
GROWS = 136
LOADS = 4
LATE = 1024
RELAY = 5
F32 = jnp.float32
BF16 = jnp.bfloat16
LONG = pl.CostEstimate(flops=60 * 10**9, bytes_accessed=1 << 20, transcendentals=0)
SHORT = pl.CostEstimate(flops=5 * 10**9, bytes_accessed=1 << 20, transcendentals=0)
NONE = pl.CostEstimate(flops=10**6, bytes_accessed=1 << 10, transcendentals=0)
MIB = 1024 * 1024
PARAMS = pltpu.CompilerParams(vmem_limit_bytes=20 * MIB)
NN = (((1,), (0,)), ((), ()))
NT = (((1,), (1,)), ((), ()))
TN = (((0,), (0,)), ((), ()))
VMEM = pl.BlockSpec(memory_space=pltpu.VMEM)
ANY = pl.BlockSpec(memory_space=pl.ANY)
SMEM = pl.BlockSpec(memory_space=pltpu.SMEM)


def halves(value):
    high = value.astype(BF16)
    return high, (value - high.astype(F32)).astype(BF16)


def dot(a, b, dims=NN):
    return lax.dot_general(a, b, dims, preferred_element_type=F32)


def dot3(a, b, dims=NN):
    return dot(a[0], b[0], dims) + (dot(a[0], b[1], dims) + dot(a[1], b[0], dims))


def beside(a, b):
    return jnp.concatenate([a, b], axis=1)


def thirds(value):
    high = value.astype(BF16)
    rest = value - high.astype(F32)
    middle = rest.astype(BF16)
    return high, middle, (rest - middle.astype(F32)).astype(BF16)


def dot4(a, b):
    return dot(a[0], b[0]) + ((dot(a[0], b[1]) + dot(a[1], b[0])) + dot(a[0], b[2]))


def dot3_narrow(a, b):
    y = dot(a[0], beside(*b))
    return y[:, :B] + (y[:, B:] + dot(a[1], b[0]))


def dot4_narrow(a, b):
    y = dot(a[0], beside(b[0], b[1]))
    return y[:, :B] + (y[:, B:] + (dot(a[1], b[0]) + dot(a[0], b[2])))


def add_gram(g_ref, pair, top, bottom):
    product = dot(beside(*halves(top)), beside(*halves(bottom)), TN)
    g_ref[pair, :B, :] += (product[:B, :B] + product[B:, B:]) + (product[:B, B:] + product[B:, :B])
    g_ref[pair, B : B + 1, :] += jnp.sum(top * top, axis=0, keepdims=True)
    g_ref[pair, B + 1 : B + 2, :] += jnp.sum(bottom * bottom, axis=0, keepdims=True)


def gram_first_kernel(x_ref, g_ref, copy_ref, sems):
    tile = x_ref.shape[0] // LOADS
    loads = []
    for i in range(LOADS):
        rows = pl.ds(i * tile, tile)
        loads.append(pltpu.make_async_copy(x_ref.at[rows], copy_ref.at[rows], sems.at[i]))
        loads[-1].start()
    g_ref[...] = jnp.zeros_like(g_ref)
    for i in range(LOADS):
        loads[i].wait()
        for pair in range(2):
            base = 2 * B * pair
            rows = slice(i * tile, (i + 1) * tile)
            add_gram(g_ref, pair, copy_ref[rows, base : base + B], copy_ref[rows, base + B : base + 2 * B])


def gram_first(x):
    return pl.pallas_call(
        gram_first_kernel,
        in_specs=[ANY],
        out_specs=VMEM,
        out_shape=jax.ShapeDtypeStruct((2, GROWS, B), F32),
        scratch_shapes=[pltpu.VMEM(x.shape, F32), pltpu.SemaphoreType.DMA((LOADS,))],
        compiler_params=pltpu.CompilerParams(vmem_limit_bytes=52 * MIB),
        name="gram_first",
    )(x)


def gram_next_kernel(rebuild, fine, flag_ref, first_ref, last_ref, b0_ref, t1_ref, in_top_ref, in_bottom_ref, *rest):
    if rebuild:
        prev_left_ref, prev_right_ref, own_ref, other_ref, *rest = rest
    g_in_ref, *_, g_ref, t0_ref, b1_ref = rest

    @pl.when(pl.program_id(0) == 0)
    def _():
        g_ref[...] = g_in_ref[...]

    in_top, in_bottom = in_top_ref[...], in_bottom_ref[...]
    if rebuild:
        q_top = jnp.where(flag_ref[2] == 0, own_ref[...], other_ref[...])
        q_bottom = jnp.where(flag_ref[2] == 0, other_ref[...], own_ref[...])
        product, parts = (dot4_narrow, thirds) if fine else (dot3_narrow, halves)
        in_top = product(halves(beside(in_top, prev_left_ref[...])), parts(q_top))
        in_bottom = product(halves(beside(prev_right_ref[...], in_bottom)), parts(q_bottom))
    t0 = jnp.where(flag_ref[0] == 1, first_ref[...], in_top)
    b1 = jnp.where(flag_ref[1] == 1, last_ref[...], in_bottom)
    t0_ref[...] = t0
    b1_ref[...] = b1
    add_gram(g_ref, 0, t0, b0_ref[...])
    add_gram(g_ref, 1, t1_ref[...], b1)


def gram_next(flags, blocks, arrived, rebuilt, g_in, start=0, written=(), fine=True):
    rows, count = blocks[0].shape[0], arrived[0].shape[0]
    tile = max(t for t in (128, 256, 512, 896, 1024) if count % t == 0 and start % t == 0)
    offset = start // tile
    block = pl.BlockSpec((tile, B), lambda i: (i + offset, 0))
    part = pl.BlockSpec((tile, B), lambda i: (i, 0))
    half = pl.BlockSpec((2 * B, B), lambda i: (0, 0))
    gram = pl.BlockSpec((2, GROWS, B), lambda i: (0, 0, 0))
    extra = [block, block, half, half] if rebuilt else []
    in_specs = [SMEM] + [block] * 4 + [part] * 2 + extra + [gram] + [ANY] * len(written)
    return pl.pallas_call(
        functools.partial(gram_next_kernel, bool(rebuilt), fine),
        grid=(count // tile,),
        in_specs=in_specs,
        out_specs=[gram, block, block],
        out_shape=[jax.ShapeDtypeStruct((2, GROWS, B), F32)] + [jax.ShapeDtypeStruct((rows, B), F32)] * 2,
        input_output_aliases={len(in_specs) - 2 + i: 1 + i for i in range(len(written))},
        compiler_params=PARAMS,
        cost_estimate=LONG if count == rows else NONE,
        name="gram_next",
    )(flags, *blocks, *arrived, *rebuilt, g_in, *written)


def polar_kernel(terms, swap, share, load, flag_ref, *refs):
    g_refs, refs = refs[:terms], refs[terms:]
    if load:
        x_ref, q_ref, copy_ref, sem = refs
        loading = pltpu.make_async_copy(x_ref, copy_ref, sem)
        loading.start()
    else:
        q_ref, *share_refs = refs
    total = g_refs[0][...]
    for g_ref in g_refs[1:]:
        total = total + g_ref[...]
    eye = (lax.broadcasted_iota(jnp.int32, (B, B), 0) == lax.broadcasted_iota(jnp.int32, (B, B), 1)).astype(F32)
    chains = []
    for pair in range(2):
        gram = total[pair, :B]
        norm_top = jnp.transpose(jnp.broadcast_to(total[pair, B : B + 1], (B, B)))
        norm_bottom = jnp.broadcast_to(total[pair, B + 1 : B + 2], (B, B))
        differ = norm_top - norm_bottom
        both = norm_top + norm_bottom + EPS
        radius = jnp.sqrt(differ * differ + 4.0 * gram * gram)
        denominator = differ * differ + jnp.abs(differ) * radius + DAMPING * both * both
        coupling = -2.0 * gram * differ / denominator
        scale = lax.rsqrt(1.0 + jnp.sum(coupling * coupling, keepdims=True))
        chains.append(beside(eye, coupling) * scale)
        chains.append(beside(-jnp.transpose(coupling), eye) * scale)

    def iterate(_, chains):
        parts = [thirds(chain) for chain in chains]
        inner = []
        for h, m, l in parts:
            y = dot(h, jnp.concatenate([h, m], axis=0), NT)
            cross = y[:, B:] + dot(h, l, NT)
            inner.append(thirds(y[:, :B] + (dot(m, m, NT) + (cross + jnp.transpose(cross)))))
        turned = []
        for (ih, im, il), (h, m, l) in zip(inner, parts):
            main, rest = dot(beside(ih, im), jnp.concatenate([h, h], axis=0)), beside(ih, im)
            rest = dot(rest, jnp.concatenate([m, m], axis=0)) + dot(beside(ih, il), jnp.concatenate([l, h], axis=0))
            turned.append(main + rest)
        return tuple(1.5 * chain - 0.5 * y for chain, y in zip(chains, turned))

    chains = lax.fori_loop(0, ITERS, iterate, tuple(chains), unroll=ITERS // 3)
    for half in range(2):
        rows = pl.ds(half * B, B)
        top, bottom = chains[half][:, :B], chains[half][:, B:]
        if share == 1:
            share_refs[0][rows, :] = jnp.where(flag_ref[2] == 0, chains[2 + half][:, :B], bottom)
        if share == 2:
            share_refs[0][rows, :], share_refs[1][rows, :] = chains[2 + half][:, :B], bottom
        if swap:
            first = flag_ref[0] == 1
            top, bottom = jnp.where(first, bottom, top), jnp.where(first, top, bottom)
        q_ref[0, rows, :] = beside(top, bottom)
        q_ref[1, rows, :] = chains[2 + half]
    if load:
        loading.wait()


def polar(flags, grams, swap=True, share=0, load=()):
    half = jax.ShapeDtypeStruct((2 * B, B), F32)
    return pl.pallas_call(
        functools.partial(polar_kernel, len(grams), swap, share, len(load)),
        in_specs=[SMEM] + [VMEM] * len(grams) + [ANY] * len(load),
        out_specs=[VMEM] * (1 + share + len(load)),
        out_shape=[jax.ShapeDtypeStruct((2, 2 * B, 2 * B), F32)]
        + [half] * share
        + [jax.ShapeDtypeStruct(x.shape, F32) for x in load],
        scratch_shapes=[pltpu.SemaphoreType.DMA] * len(load),
        compiler_params=pltpu.CompilerParams(vmem_limit_bytes=(40 if load else 20) * MIB),
        cost_estimate=SHORT,
        name="polar",
    )(flags, *grams, *load)


def turned(refs, q, rows):
    x = halves(beside(refs[0][rows, :], refs[1][rows, :]))
    return dot4(x, q) if len(q) == 3 else dot3(x, q)


def tiles(count, *cuts):
    bounds = [0, *cuts, count]
    return [pl.ds(i, min(TILE, hi - i)) for lo, hi in zip(bounds, bounds[1:]) for i in range(lo, hi, TILE)]


def rotate_kernel(early, fine, t0_ref, b0_ref, t1_ref, b1_ref, q_ref, t1n_ref, left_ref, right_ref, b0n_ref, *parts):
    count = t0_ref.shape[0]
    q = [(thirds if fine else halves)(q_ref[pair]) for pair in range(2)]
    for rows in tiles(count, *([early] if parts else [])):
        top = turned((t0_ref, b0_ref), q[0], rows)
        bottom = turned((t1_ref, b1_ref), q[1], rows)
        t1n_ref[rows, :], left_ref[rows, :] = top[:, :B], top[:, B:]
        right_ref[rows, :], b0n_ref[rows, :] = bottom[:, :B], bottom[:, B:]
        if parts:
            late = int(rows.start >= early)
            part = pl.ds(rows.start - late * early, rows.size)
            parts[late][part, :], parts[2 + late][part, :] = top[:, :B], bottom[:, B:]


def rotate(blocks, q, early=0, fine=True):
    count = blocks[0].shape[0]
    sizes = [count] * 4 + ([early, count - early] * 2 if early else [])
    return pl.pallas_call(
        functools.partial(rotate_kernel, early, fine),
        in_specs=[VMEM] * 5,
        out_specs=[VMEM] * len(sizes),
        out_shape=[jax.ShapeDtypeStruct((size, B), F32) for size in sizes],
        compiler_params=pltpu.CompilerParams(vmem_limit_bytes=16 * MIB),
        cost_estimate=SHORT,
        name="rotate",
    )(*blocks, q)


def rotate_last_kernel(t0_ref, b0_ref, t1_ref, b1_ref, q_ref, out_ref, held_ref, sems):
    q = [halves(q_ref[pair]) for pair in range(2)]
    stores = []
    for i in range(sems.shape[0]):
        tile = out_ref.shape[0] // sems.shape[0]
        rows = pl.ds(i * tile, tile)
        held_ref[rows, : 2 * B] = turned((t0_ref, b0_ref), q[0], rows)
        held_ref[rows, 2 * B :] = turned((t1_ref, b1_ref), q[1], rows)
        stores.append(pltpu.make_async_copy(held_ref.at[rows], out_ref.at[rows], sems.at[i]))
        stores[-1].start()
    for store in stores:
        store.wait()


def rotate_last(blocks, q):
    count = blocks[0].shape[0]
    return pl.pallas_call(
        rotate_last_kernel,
        in_specs=[VMEM] * 5,
        out_specs=ANY,
        out_shape=jax.ShapeDtypeStruct((count, 4 * B), F32),
        scratch_shapes=[pltpu.VMEM((count, 4 * B), F32), pltpu.SemaphoreType.DMA((8,))],
        compiler_params=pltpu.CompilerParams(vmem_limit_bytes=16 * MIB),
        name="rotate_last",
    )(*blocks, q)


def rotate_part_kernel(columns, x_ref, q_ref, *outs):
    for pair in range(2):
        q = thirds(q_ref[pair, :, columns[pair] : columns[pair] + B])
        outs[pair][...] = dot4_narrow(halves(x_ref[:, 2 * B * pair : 2 * B * (pair + 1)]), q)


def rotate_part(x, q, columns):
    rows = x.shape[0]
    tile = min(TILE, rows)
    block = pl.BlockSpec((tile, B), lambda i: (i, 0))
    return pl.pallas_call(
        functools.partial(rotate_part_kernel, columns),
        grid=(rows // tile,),
        in_specs=[pl.BlockSpec((tile, 4 * B), lambda i: (i, 0)), pl.BlockSpec((2, 2 * B, 2 * B), lambda i: (0, 0, 0))],
        out_specs=[block] * 2,
        out_shape=[jax.ShapeDtypeStruct((rows, B), F32)] * 2,
        compiler_params=PARAMS,
        name="rotate_part",
    )(x, q)


def shifted(value, steps):
    count = lax.axis_size("pair")
    initial, last = (max(0, -steps), min(count, count - steps))
    return lax.ppermute(value, "pair", [(source, source + steps) for source in range(initial, last)])


def row_terms(g, relayed):
    rows, pairs = lax.axis_size("row"), lax.axis_size("pair")
    part = g + lax.ppermute(g, "row", [(r, r ^ 1) for r in range(rows)])
    if not relayed:
        return [part, lax.ppermute(part, "row", [(r, r ^ 2) for r in range(rows)])]
    both = ("pair", "row")
    relay = {0: RELAY, pairs - 1: pairs - 1 - RELAY}
    here = [p * rows + r for p in range(pairs) if p not in relay for r in range(rows)]
    ends = [(p * rows + r, via * rows + r) for p, via in relay.items() for r in range(rows)]
    hop = lax.ppermute(part, both, [(end, via ^ 2) for end, via in ends])
    direct = lax.ppermute(part, both, [(i, i ^ 2) for i in here])
    return [part, direct, lax.ppermute(hop, both, [(via, end) for end, via in ends])]


def sent(half):
    rows, pairs = lax.axis_size("row"), lax.axis_size("pair")
    right = [(p * rows + r, (p + 1) * rows + r) for p in range(pairs - 1) for r in range(0, rows, 2)]
    left = [(p * rows + r, (p - 1) * rows + r) for p in range(1, pairs) for r in range(1, rows, 2)]
    return lax.ppermute(half, ("pair", "row"), right + left)


def with_other(own, block):
    own, block = lax.optimization_barrier((own, block))
    return (own, lax.ppermute(own, "row", [(r, r ^ 1) for r in range(lax.axis_size("row"))])), block


def per_device(factor):
    position = lax.axis_index("pair")
    ends = [position == 0, position == lax.axis_size("pair") - 1, lax.axis_index("row") % 2 == 1]
    flags = jnp.stack(ends).astype(jnp.int32)
    ordered = jnp.stack(ends[:2] + [position < 0]).astype(jnp.int32)
    zero = jnp.zeros((2, GROWS, B), F32)

    count = factor.shape[0]
    early = count - LATE
    q, factor = polar(flags, row_terms(gram_first(factor), False), load=(factor,))
    left, right = rotate_part(factor, q, (B, 0))
    arrived = (shifted(right, 1), shifted(left, -1))
    t1, b0 = rotate_part(factor, q, (0, B))
    ahead = (shifted(t1, 1), shifted(b0, -1))

    g, t0, b1 = gram_next(flags, (left, right, b0, t1), arrived, (), zero)
    q, half_right, half_left = polar(flags, row_terms(g, True), share=2)
    rebuilt = (left, right, shifted(half_right, 1), shifted(half_left, -1))
    t1, left, right, b0, t1_early, t1_late, b0_early, b0_late = rotate([t0, b0, t1, b1], q, early)
    arrived, ahead = ahead, (shifted(t1_early, 1), shifted(b0_early, -1))

    g, t0, b1 = gram_next(ordered, (left, right, b0, t1), arrived, rebuilt, zero)
    q, half = polar(flags, row_terms(g, True), share=1)
    half = sent(half)
    before = (left, right)
    (t1_late, b0_late), q = lax.optimization_barrier(((t1_late, b0_late), q))
    arrived = (shifted(t1_late, 1), shifted(b0_late, -1))
    t1, left, right, b0 = rotate([t0, b0, t1, b1], q, fine=False)
    halves_q, left = with_other(half, left)
    rebuilt = (*before, *halves_q)

    g, t0, b1 = gram_next(flags, (left, right, b0, t1), ahead, rebuilt, zero, fine=False)
    g, t0, b1 = gram_next(flags, (left, right, b0, t1), arrived, rebuilt, g, early, (t0, b1), fine=False)
    (q,) = polar(flags, row_terms(g, False), swap=False)
    return rotate_last([t0, b0, t1, b1], q)


def solution(mesh):
    placed = (P("row", "pair"),)
    return jax.shard_map(
        per_device, mesh=mesh, in_specs=placed, out_specs=P("row", "pair"), check_vma=False
    )
```
